256 devices in a mesh: atom: 16 (over z_hi, x, core), row: 4 (over z_lo), col: 4 (over y).
Axes of the slice: x: 4, y: 4, z: 8 (z_hi: 2, z_lo: 4; z = z_hi * 4 + z_lo), core: 2. Of those that a mesh axis runs over, the one named last changes fastest.
Arguments:
- atom_feats: bfloat16 [65536, 128], P(('atom', 'row', 'col')), may hold values from -6 to 6
- atom_to_token: int32 [65536], P(('atom', 'row', 'col')), may hold values from 0 to 8191, as said below
- window_start: int32 [2048], P(('atom', 'row', 'col')), may hold values from -64 to 65472, as said below
- atom_bias: bfloat16 [65536, 512], P(('atom', 'row', 'col')), may hold values from -240 to 240
- token_single: bfloat16 [8192, 768], P(('atom', 'row', 'col')), may hold values from -6 to 6
- token_mask: int32 [8192], replicated, may hold values from 0 to 1, as said below
- pair_bias: bfloat16 [16, 8192, 8192], P('atom', 'row', 'col'), may hold values from -240 to 240
- w_atom: bfloat16 [128, 512], replicated, may hold values from -0.5 to 0.5
- w_atom_out: bfloat16 [128, 128], replicated, may hold values from -0.5 to 0.5
- w_to_token: bfloat16 [128, 768], replicated, may hold values from -0.5 to 0.5
- w_token: bfloat16 [768, 3072], replicated, may hold values from -0.21875 to 0.21875
- w_out: bfloat16 [768, 768], P(None, 'col'), may hold values from -0.21875 to 0.21875
Outputs:
- atom_update: bfloat16 [65536, 128], P(('atom', 'row', 'col'))
- token_update: bfloat16 [8192, 768], P(('row', 'atom'), 'col')
The draws below stay inside these ranges and needn't reach their ends.
Inputs may be any that keep to these rules, and one draw needn't show every extreme that they name: `atom_to_token`: never falls along the atoms; every token owns 1 to 24 atoms and some token of every device's block owns exactly 24; the tokens t with t // 32 = i own exactly the atoms n with n // 256 = i. `window_start`: block b's window starts between 32 * b - 64 and 32 * b - 32. `token_mask`: ones on a leading run of tokens, zeros after it; at least 4096 ones.
All inputs are finite; a program needn't handle non-finite values.
Results may differ from the reference program's by a relative error of at most 0.029.
Values may be sent and summed in bfloat16 or wider, within the bound.
A program may use at most 128 MiB of HBM per device.

```python
import jax
import jax.numpy as jnp
from jax import lax

CA = 128
AH = 4
CT = 768
TH = 16
QB = 32
KW = 128
HALO = 64
ATOM_DEV = 256
TOK_DEV = 32
ATOMS = 65536
TOKENS = 8192
HD = 48


def draw_atom_to_token(key, part):
    key = jax.random.fold_in(key, 1)
    blocks = ATOMS // ATOM_DEV
    others = TOK_DEV - 1
    rest = ATOM_DEV - 24
    slot = jnp.arange(others, dtype=jnp.int32)
    start_counts = rest // others + (slot < rest % others).astype(jnp.int32)
    counts = jnp.broadcast_to(start_counts[None, :], (blocks, others))

    def mix_step(step, held):
        sub = jax.random.fold_in(key, step + 100)
        source = jax.random.randint(jax.random.fold_in(sub, 1), (blocks, 1), 0, others)
        target = jax.random.randint(jax.random.fold_in(sub, 2), (blocks, 1), 0, others)
        amount = jax.random.randint(jax.random.fold_in(sub, 3), (blocks, 1), 0, 13)
        from_count = jnp.take_along_axis(held, source, axis=1)
        to_count = jnp.take_along_axis(held, target, axis=1)
        amount = jnp.minimum(amount, jnp.minimum(from_count - 1, 24 - to_count))
        moved_out = amount * (slot[None, :] == source).astype(jnp.int32)
        moved_in = amount * (slot[None, :] == target).astype(jnp.int32)
        return held - moved_out + moved_in
    counts = lax.fori_loop(0, 4 * TOK_DEV, mix_step, counts)
    place = jax.random.randint(jax.random.fold_in(key, 7), (blocks, 1), 0, TOK_DEV)
    full = jnp.arange(TOK_DEV, dtype=jnp.int32)[None, :]
    shifted = jnp.clip(full - (full > place).astype(jnp.int32), 0, others - 1)
    values = jnp.take_along_axis(counts, jnp.broadcast_to(shifted, (blocks, TOK_DEV)), axis=1)
    owned = jnp.where(full == place, 24, values)
    ends = jnp.cumsum(owned, axis=1)
    atom_slot = jnp.arange(ATOM_DEV, dtype=jnp.int32)
    local = jnp.sum((ends[:, :, None] <= atom_slot[None, None, :]).astype(jnp.int32), axis=1)
    token = local + TOK_DEV * jnp.arange(blocks, dtype=jnp.int32)[:, None]
    return token.reshape(ATOMS).astype(jnp.int32)


def draw_window_start(key, part):
    key = jax.random.fold_in(key, 2)
    blocks = ATOMS // QB
    jitter = jax.random.randint(key, (blocks,), -16, 17)
    jitter = jitter.at[0].set(-16).at[blocks - 1].set(16)
    return (QB * jnp.arange(blocks, dtype=jnp.int32) - 48 + jitter).astype(jnp.int32)


def draw_atom_bias(key, part):
    key = jax.random.fold_in(key, 3)
    table = jnp.clip(jax.random.normal(key, (ATOMS, AH, KW), jnp.float32), -6.0, 6.0)
    return table.reshape(ATOMS, AH * KW).astype(jnp.bfloat16)


def draw_token_mask(key, part):
    key = jax.random.fold_in(key, 5)
    live = jax.random.randint(key, (), TOKENS // 2, TOKENS)
    return (jnp.arange(TOKENS, dtype=jnp.int32) < live).astype(jnp.int32)


def draw_pair_bias(key, part):
    key = jax.random.fold_in(key, 4)
    table = jnp.clip(jax.random.normal(key, (TH, TOKENS, TOKENS), jnp.float32), -6.0, 6.0)
    return table.astype(jnp.bfloat16)


def levels(rng, dims, pieces, least, high):
    def one(dim, blocks):
        steps = jax.random.uniform(jax.random.fold_in(jax.random.fold_in(rng, 6), dim), (blocks,), jnp.float32, least / len(pieces), high / len(pieces))
        return jnp.repeat(jnp.exp(steps), dims[dim] // blocks).reshape((-1,) + (1,) * (len(dims) - dim - 1))

    gain = one(*pieces[0])
    for cut in pieces[1:]:
        gain = gain * one(*cut)
    return gain


def normal_values(stream_key, dims, scale, reach, split=(), held_as=jnp.bfloat16):
    drawn = jax.random.normal(stream_key, dims, jnp.float32) * scale
    if len(split) > 0:
        drawn = levels(stream_key, dims, split, -0.22, 0.18) * drawn
    return jnp.clip(drawn, min=-reach, max=reach).astype(held_as)


def setup_inputs(seed: int = 0) -> dict:
    streams_of = jax.random.split(jax.random.key(seed), 13)
    atom_feats = normal_values(streams_of[0], (ATOMS, CA), 1.0, 6.0, ((0, 256),))
    atom_to_token = draw_atom_to_token(jax.random.fold_in(streams_of[12], 71), 0)
    window_start = draw_window_start(jax.random.fold_in(streams_of[12], 71), 0)
    atom_bias = draw_atom_bias(jax.random.fold_in(streams_of[12], 71), 0)
    token_single = normal_values(streams_of[4], (TOKENS, CT), 1.0, 6.0, ((0, 256),))
    token_mask = draw_token_mask(jax.random.fold_in(streams_of[12], 71), 0)
    pair_bias = draw_pair_bias(jax.random.fold_in(streams_of[12], 71), 0)
    w_atom = normal_values(streams_of[7], (CA, 4 * CA), CA ** -0.5, 0.5)
    w_atom_out = normal_values(streams_of[8], (CA, CA), CA ** -0.5, 0.5)
    w_to_token = normal_values(streams_of[9], (CA, CT), CA ** -0.5, 0.5)
    w_token = normal_values(streams_of[10], (CT, 4 * CT), CT ** -0.5, 0.21875)
    w_out = normal_values(streams_of[11], (CT, CT), CT ** -0.5, 0.21875, ((1, 4),))
    return dict(atom_feats=atom_feats, atom_to_token=atom_to_token, window_start=window_start, atom_bias=atom_bias, token_single=token_single, token_mask=token_mask, pair_bias=pair_bias, w_atom=w_atom, w_atom_out=w_atom_out, w_to_token=w_to_token, w_token=w_token, w_out=w_out)


EPS = 1e-05
NEG = -1e+30

def layer_norm(values):
    values = values.astype(jnp.float32)
    centre = values - lax.optimization_barrier(jnp.mean(values, axis=-1, keepdims=True))
    spread = lax.optimization_barrier(jnp.mean(centre * centre, axis=-1, keepdims=True))
    return centre * lax.rsqrt(spread + EPS)

def window_attend(query, wide, offset, window_start, total, atom_bias, gate, w_atom_out):
    blocks = query.shape[0] // QB
    width = query.shape[1]
    head_dim = width // AH
    span = jnp.arange(KW, dtype=jnp.int32)
    rows = offset[:, None] + span[None, :]
    keyed = wide[rows]
    placed = window_start[:, None] + span[None, :]
    valid = (placed >= 0) & (placed < total)
    keys = keyed[:, :, :width].reshape(blocks, KW, AH, head_dim).astype(jnp.float32)
    values = keyed[:, :, width:].reshape(blocks, KW, AH, head_dim).astype(jnp.float32)
    queries = query.reshape(blocks, QB, AH, head_dim).astype(jnp.float32)
    scores = jnp.einsum('bqhd,bkhd->bqhk', queries, keys) * head_dim ** (-0.5)
    scores = scores + atom_bias.reshape(blocks, QB, AH, KW).astype(jnp.float32)
    scores = jnp.where(valid[:, None, None, :], scores, NEG)
    top = lax.optimization_barrier(jnp.max(scores, axis=-1, keepdims=True))
    expo = jnp.exp(scores - top)
    weights = (expo / lax.optimization_barrier(jnp.sum(expo, axis=-1, keepdims=True))).astype(jnp.bfloat16)
    mixed = jnp.einsum('bqhk,bkhd->bqhd', weights.astype(jnp.float32), values)
    gated = (mixed.reshape(blocks * QB, width) * gate).astype(jnp.bfloat16)
    return jnp.dot(gated, w_atom_out, preferred_element_type=jnp.float32)

def reference(atom_feats, atom_to_token, window_start, atom_bias, token_single, token_mask, pair_bias, w_atom, w_atom_out, w_to_token, w_token, w_out):
    normed = layer_norm(atom_feats).astype(jnp.bfloat16)
    proj = jnp.dot(normed, w_atom, preferred_element_type=jnp.float32)
    query = proj[:, :CA].astype(jnp.bfloat16)
    pairs = proj[:, CA:3 * CA].astype(jnp.bfloat16)
    gate = jax.nn.sigmoid(proj[:, 3 * CA:])
    wide = jnp.pad(pairs, ((HALO, HALO), (0, 0)))
    change = window_attend(query, wide, window_start + HALO, window_start, ATOMS, atom_bias, gate, w_atom_out)
    atom_update = change.astype(jnp.bfloat16)
    acted = (atom_feats.astype(jnp.float32) + change).astype(jnp.bfloat16)
    hidden = jax.nn.relu(jnp.dot(acted, w_to_token, preferred_element_type=jnp.float32)).astype(jnp.bfloat16)
    sums = jax.ops.segment_sum(hidden.astype(jnp.float32), atom_to_token, num_segments=TOKENS)
    counts = jax.ops.segment_sum(jnp.ones((ATOMS,), jnp.float32), atom_to_token, num_segments=TOKENS)
    single = token_single.astype(jnp.float32) + sums / counts[:, None]
    normed_tokens = layer_norm(single).astype(jnp.bfloat16)
    head_data = jnp.dot(normed_tokens, w_token, preferred_element_type=jnp.float32).astype(jnp.bfloat16)
    head_data = head_data.reshape(TOKENS, TH, 4, HD)
    live = token_mask > 0

    def one_head(index):
        part = lax.dynamic_index_in_dim(head_data, index, 1, keepdims=False)
        bias = lax.dynamic_index_in_dim(pair_bias, index, 0, keepdims=False).astype(jnp.float32)
        scores = jnp.dot(part[:, 0], part[:, 1].T, preferred_element_type=jnp.float32) * HD ** (-0.5) + bias
        scores = jnp.where(live[None, :], scores, NEG)
        top = lax.optimization_barrier(jnp.max(scores, axis=-1, keepdims=True))
        expo = jnp.exp(scores - top)
        total = lax.optimization_barrier(jnp.sum(expo, axis=-1, keepdims=True))
        mixed = jnp.dot(expo.astype(jnp.bfloat16), part[:, 2], preferred_element_type=jnp.float32)
        return mixed / total * jax.nn.sigmoid(part[:, 3].astype(jnp.float32))
    heads = lax.map(one_head, jnp.arange(TH, dtype=jnp.int32))
    attended = heads.transpose(1, 0, 2).reshape(TOKENS, CT).astype(jnp.bfloat16)
    token_update = jnp.dot(attended, w_out, preferred_element_type=jnp.float32).astype(jnp.bfloat16)
    return (atom_update, token_update)
```

```python
import functools

import jax
import jax.numpy as jnp
from jax import lax
from jax.experimental import pallas as pl
from jax.experimental.pallas import tpu as pltpu
from jax.sharding import PartitionSpec as P

AH = 4
QB = 32
KW = 128
HALO = 64
HD = 48
EPS = 1e-05
NEG = -1e30
BF = jnp.bfloat16
F32 = jnp.float32
MESH = pl.DeviceIdType.MESH
VMEM = pl.BlockSpec(memory_space=pltpu.VMEM)
SMEM = pl.BlockSpec(memory_space=pltpu.SMEM)
NT = (((1,), (1,)), ((), ()))


def layer_norm(values):
    centre = values - jnp.mean(values, axis=-1, keepdims=True)
    spread = jnp.mean(centre * centre, axis=-1, keepdims=True)
    return (centre * lax.rsqrt(spread + EPS)).astype(BF)


def dot(a, b):
    return jnp.dot(a, b, preferred_element_type=F32)


def iota(shape, dim):
    return lax.broadcasted_iota(jnp.int32, shape, dim)


def place():
    return lax.axis_index("atom"), lax.axis_index("row"), lax.axis_index("col")


def atom_kernel(
    all_atoms,
    start_ref,
    feats_ref,
    before_ref,
    after_ref,
    member_ref,
    bias_ref,
    single_ref,
    mask_ref,
    w_atom_ref,
    w_atom_out_ref,
    w_to_token_ref,
    w_token_ref,
    update_ref,
    qg_ref,
    kv_ref,
):
    a, r, c = place()
    device = (a * lax.axis_size("row") + r) * lax.axis_size("col") + c
    rows, width = feats_ref.shape
    toks = single_ref.shape[0]
    heads = qg_ref.shape[0]
    feats = feats_ref[...].astype(F32)
    wide = jnp.concatenate([before_ref[...].astype(F32), feats, after_ref[...].astype(F32)], axis=0)
    proj = dot(layer_norm(wide), w_atom_ref[...])
    queries = proj[HALO : HALO + rows, :width].astype(BF)
    pairs = proj[:, width : 3 * width].astype(BF)
    gate = jax.nn.sigmoid(proj[HALO : HALO + rows, 3 * width :])
    part = width // AH
    reach = KW + QB
    lane_head = iota((QB, width), 1) // part
    ahead = iota((KW, reach), 1) - iota((KW, reach), 0)
    slot = iota((1, KW), 1)
    blocks = []
    for b in range(rows // QB):
        start = start_ref[b]
        shift = start - (device * rows + QB * b) + HALO
        pick = jnp.where(ahead == shift, 1.0, 0.0).astype(BF)
        keyed = dot(pick, pairs[QB * b : QB * b + reach]).astype(BF)
        query = queries[QB * b : QB * (b + 1)]
        stacked = jnp.concatenate(
            [jnp.where(lane_head == h, query, jnp.zeros_like(query)) for h in range(AH)], axis=0
        )
        scores = lax.dot_general(stacked, keyed[:, :width], NT, preferred_element_type=F32)
        bias = jnp.concatenate(
            [bias_ref[QB * b : QB * (b + 1), KW * h : KW * (h + 1)] for h in range(AH)], axis=0
        )
        scores = scores * part ** (-0.5) + bias.astype(F32)
        placed = start + slot
        scores = jnp.where((placed >= 0) & (placed < all_atoms), scores, NEG)
        expo = jnp.exp(scores - jnp.max(scores, axis=-1, keepdims=True))
        weights = (expo / jnp.sum(expo, axis=-1, keepdims=True)).astype(BF)
        mixed = dot(weights, keyed[:, width:])
        block = jnp.zeros((QB, width), F32)
        for h in range(AH):
            block = jnp.where(lane_head == h, mixed[QB * h : QB * (h + 1)], block)
        blocks.append(block)
    gated = (jnp.concatenate(blocks, axis=0) * gate).astype(BF)
    change = dot(gated, w_atom_out_ref[...])
    update_ref[...] = change.astype(BF)
    acted = (feats + change).astype(BF)
    hidden = jnp.maximum(dot(acted, w_to_token_ref[...]), 0.0).astype(BF)
    local = member_ref[...] - device * toks
    member = jnp.where(local == iota((toks, rows), 0), 1.0, 0.0)
    sums = dot(member.astype(BF), hidden)
    counts = jnp.sum(member, axis=1, keepdims=True)
    single = single_ref[...].astype(F32) + sums / counts
    head_data = dot(layer_norm(single), w_token_ref[...]).astype(BF)
    span = 8 * HD
    stacked = jnp.concatenate(
        [head_data[:, span * p : span * (p + 1)] for p in range(heads // 2)], axis=0
    )
    source, target = iota((span, 512), 0), iota((span, 512), 1)
    lane = target % 128
    kind = (target // 128) % 2
    base = (target // 256) * 4 * HD + kind * HD
    first = base + lane
    second = base + jnp.where(kind == 0, 2 * HD, 0) + lane
    wanted = jnp.where(lane < HD, first, jnp.where(lane < 2 * HD, second, -1))
    spread = dot(stacked, jnp.where(source == wanted, 1.0, 0.0).astype(BF))
    live = jnp.sum(jnp.sum(mask_ref[...], axis=0, keepdims=True), axis=1, keepdims=True)
    token = device * toks + iota((toks, 128), 0)
    lanes = iota((toks, 128), 1)
    masked = jnp.where(token < live, 0.0, NEG)
    for h in range(heads):
        rows_h = slice(toks * (h // 2), toks * (h // 2 + 1))
        at = 256 * (h % 2)
        qg = jnp.where(lanes == 2 * HD, 1.0, spread[rows_h, at : at + 128])
        kv = jnp.where(lanes == 2 * HD, masked, spread[rows_h, at + 128 : at + 256])
        kv = jnp.where(lanes == 2 * HD + 1, 1.0, kv)
        qg_ref[h] = qg.astype(BF)
        kv_ref[h] = kv.astype(BF)


def exchange_kernel(qg_ref, kv_ref, qall_ref, kall_ref, send, q_sem, k_sem, g_send, gq_sem, gk_sem):
    a, r, c = place()
    n_atom, n_row, n_col = (lax.axis_size(x) for x in ("atom", "row", "col"))
    group_q, group_k = n_atom // n_row, n_atom // n_col
    barrier = pltpu.get_barrier_semaphore()

    def signal(to):
        pl.semaphore_signal(barrier, inc=1, device_id=to, device_id_type=MESH)

    own_q = a // group_q == r
    own_k = a // group_k == c

    def greet(i, carry):
        source = (group_q * r + i // n_row, i % n_row, c)

        @pl.when(jnp.logical_not((source[0] == a) & (source[1] == r)))
        def _():
            signal(source)

        source_k = (group_k * c + i // n_col, r, i % n_col)

        @pl.when(jnp.logical_not((source_k[0] == a) & (source_k[2] == c)))
        def _():
            signal(source_k)

        return carry

    lax.fori_loop(0, n_atom, greet, 0)
    for step in range(1, n_col):
        signal((a, r, lax.rem(c + step, n_col)))
    for step in range(1, n_row):
        signal((a, lax.rem(r + step, n_row), c))
    count = 2 * n_atom + (n_col - 1) + (n_row - 1)
    pl.semaphore_wait(barrier, count - own_q.astype(jnp.int32) - own_k.astype(jnp.int32))

    q_slot = lax.rem(a, group_q) * n_row + r
    k_slot = (lax.rem(a, group_k), r, c)

    def q_copy(to):
        return pltpu.make_async_remote_copy(
            src_ref=qg_ref.at[to],
            dst_ref=qall_ref.at[q_slot, c],
            send_sem=send.at[0, to],
            recv_sem=q_sem.at[q_slot],
            device_id=(to, a // group_q, c),
            device_id_type=MESH,
        )

    def k_copy(to):
        return pltpu.make_async_remote_copy(
            src_ref=kv_ref.at[to],
            dst_ref=kall_ref.at[k_slot],
            send_sem=send.at[1, to],
            recv_sem=k_sem.at[lax.rem(a, group_k) * n_col + c],
            device_id=(to, r, a // group_k),
            device_id_type=MESH,
        )

    def start(i, carry):
        to = lax.rem(a + i, n_atom)
        self_q = own_q & (to == a)
        self_k = own_k & (to == a)

        @pl.when(jnp.logical_not(self_q))
        def _():
            q_copy(to).start()

        @pl.when(self_q)
        def _():
            pltpu.make_async_copy(qg_ref.at[to], qall_ref.at[q_slot, c], q_sem.at[q_slot]).start()

        @pl.when(jnp.logical_not(self_k))
        def _():
            k_copy(to).start()

        @pl.when(self_k)
        def _():
            pltpu.make_async_copy(
                kv_ref.at[to], kall_ref.at[k_slot], k_sem.at[lax.rem(a, group_k) * n_col + c]
            ).start()

        return carry

    lax.fori_loop(0, n_atom, start, 0)

    def arrive_q(i, carry):
        pltpu.make_async_copy(qg_ref.at[0], qall_ref.at[i, c], q_sem.at[i]).wait()
        return carry

    lax.fori_loop(0, n_atom, arrive_q, 0)

    def gather_q(step):
        to = lax.rem(c + step, n_col)
        mine = qall_ref.at[:, c]
        return pltpu.make_async_remote_copy(
            src_ref=mine,
            dst_ref=mine,
            send_sem=g_send.at[0, step],
            recv_sem=gq_sem.at[step],
            device_id=(a, r, to),
            device_id_type=MESH,
        )

    def gather_k(step):
        to = lax.rem(r + step, n_row)
        mine = kall_ref.at[:, r]
        return pltpu.make_async_remote_copy(
            src_ref=mine,
            dst_ref=mine,
            send_sem=g_send.at[1, step],
            recv_sem=gk_sem.at[step],
            device_id=(a, to, c),
            device_id_type=MESH,
        )

    for step in range(1, n_col):
        gather_q(step).start()

    def arrive_k(i, carry):
        pltpu.make_async_copy(
            kv_ref.at[0], kall_ref.at[i // n_col, r, i % n_col], k_sem.at[i]
        ).wait()
        return carry

    lax.fori_loop(0, n_atom, arrive_k, 0)
    for step in range(1, n_row):
        gather_k(step).start()
    for step in range(1, n_col):
        gather_q(step).wait()
    for step in range(1, n_row):
        gather_k(step).wait()

    def sent(to, carry):
        @pl.when(jnp.logical_not(own_q & (to == a)))
        def _():
            q_copy(to).wait_send()

        @pl.when(jnp.logical_not(own_k & (to == a)))
        def _():
            k_copy(to).wait_send()

        return carry

    lax.fori_loop(0, n_atom, sent, 0)


def attend_kernel(qg_ref, kv_ref, bias_ref, out_ref, score_ref, weight_ref):
    rows, keys = score_ref.shape
    chunk = 256
    lane = iota((rows, 128), 1)
    qg = qg_ref[...]
    query = jnp.where((lane < HD) | (lane == 2 * HD), qg, jnp.zeros_like(qg))
    peak = jnp.full((rows, 128), -jnp.inf, F32)
    for at in range(0, keys, chunk):
        part = lax.dot_general(query, kv_ref[at : at + chunk], NT, preferred_element_type=F32)
        part = part * HD ** (-0.5) + bias_ref[0, :, at : at + chunk].astype(F32)
        score_ref[:, at : at + chunk] = part
        for k in range(0, chunk, 128):
            peak = jnp.maximum(peak, part[:, k : k + 128])
    top = jnp.max(peak, axis=1, keepdims=True)
    for at in range(0, keys, chunk):
        weight_ref[:, at : at + chunk] = jnp.exp(score_ref[:, at : at + chunk] - top).astype(BF)
    mixed = dot(weight_ref[...], kv_ref[...])
    total = mixed[:, 2 * HD + 1 : 2 * HD + 2]
    high = top.astype(BF).astype(F32)
    middle = (top - high).astype(BF).astype(F32)
    low = top - high - middle
    total_high = total.astype(BF).astype(F32)
    result = mixed
    for at, value in enumerate((high, middle, low, total_high, total - total_high)):
        result = jnp.where(lane == at, value, result)
    out_ref[...] = result.astype(BF)


def merge_kernel(
    part_ref, qg_ref, w_ref, out_ref, got_ref, head_ref, all_ref, m_send, m_recv, h_send, h_recv
):
    a, r, c = place()
    n_atom, n_col = lax.axis_size("atom"), lax.axis_size("col")
    group = n_atom // n_col
    barrier = pltpu.get_barrier_semaphore()

    def signal(to):
        pl.semaphore_signal(barrier, inc=1, device_id=to, device_id_type=MESH)

    own = a // group == c
    for step in range(1, n_col):
        signal((a, r, lax.rem(c + step, n_col)))

    def greet(i, carry):
        @pl.when(jnp.logical_not(own & (i == a)))
        def _():
            signal((i, r, a // group))

        return carry

    lax.fori_loop(0, n_atom, greet, 0)
    pl.semaphore_wait(barrier, n_col - 1 + n_atom - own.astype(jnp.int32))

    def partial(step):
        to = lax.rem(c + step, n_col)
        return pltpu.make_async_remote_copy(
            src_ref=part_ref.at[to],
            dst_ref=got_ref.at[step],
            send_sem=m_send.at[step],
            recv_sem=m_recv.at[step],
            device_id=(a, r, to),
            device_id_type=MESH,
        )

    for step in range(1, n_col):
        partial(step).start()
    for step in range(1, n_col):
        partial(step).wait_recv()

    def head_copy(j, k):
        to = lax.rem(c + k, n_col)
        return pltpu.make_async_remote_copy(
            src_ref=head_ref.at[j],
            dst_ref=all_ref.at[a],
            send_sem=h_send.at[j, k],
            recv_sem=h_recv.at[a],
            device_id=(group * c + j, r, to),
            device_id_type=MESH,
        )

    rows = head_ref.shape[2]

    def one(j, carry):
        span = pl.ds(pl.multiple_of(j * rows, rows), rows)
        parts = [part_ref[c, span]] + [got_ref[step, span] for step in range(1, n_col)]
        parts = [p.astype(F32) for p in parts]
        tops = [p[:, 0:1] + p[:, 1:2] + p[:, 2:3] for p in parts]
        totals = [p[:, 3:4] + p[:, 4:5] for p in parts]
        top = functools.reduce(jnp.maximum, tops)
        scales = [jnp.exp(t - top) for t in tops]
        total = sum(s * t for s, t in zip(scales, totals))
        mixed = sum(s * p for s, p in zip(scales, parts))
        gates = jax.nn.sigmoid(qg_ref[c, span].astype(F32))
        attended = jnp.transpose(mixed / total * gates)
        head_ref[j] = attended[HD : 2 * HD].astype(BF)
        for k in range(n_col):
            if k == 0:

                @pl.when(jnp.logical_not(own & (group * c + j == a)))
                def _():
                    head_copy(j, 0).start()

                @pl.when(own & (group * c + j == a))
                def _():
                    pltpu.make_async_copy(head_ref.at[j], all_ref.at[a], h_recv.at[a]).start()

            else:
                head_copy(j, k).start()
        return carry

    lax.fori_loop(0, group, one, 0)

    def arrive(i, carry):
        pltpu.make_async_copy(head_ref.at[0], all_ref.at[i], h_recv.at[i]).wait()
        return carry

    lax.fori_loop(0, n_atom, arrive, 0)
    heads = all_ref[...].reshape(n_atom * HD, rows)
    out_ref[...] = jnp.transpose(dot(w_ref[...], heads)).astype(BF)
    for step in range(1, n_col):
        partial(step).wait_send()

    def sent(j, carry):
        for k in range(n_col):
            if k == 0:

                @pl.when(jnp.logical_not(own & (group * c + j == a)))
                def _():
                    head_copy(j, 0).wait_send()

            else:
                head_copy(j, k).wait_send()
        return carry

    lax.fori_loop(0, group, sent, 0)


def shards(
    atom_feats,
    atom_to_token,
    window_start,
    atom_bias,
    token_single,
    token_mask,
    pair_bias,
    w_atom,
    w_atom_out,
    w_to_token,
    w_token,
    w_out,
):
    rows, width = atom_feats.shape
    toks = token_single.shape[0]
    axes = ("atom", "row", "col")
    n_atom, n_row, n_col = (lax.axis_size(x) for x in axes)
    devices = n_atom * n_row * n_col
    up = [(i, (i + 1) % devices) for i in range(devices)]
    down = [(j, i) for i, j in up]
    before = lax.ppermute(atom_feats[rows - HALO :], axes, up)
    after = lax.ppermute(atom_feats[:HALO], axes, down)
    tile = jax.ShapeDtypeStruct((n_atom, toks, 128), BF)
    update, qg, kv = pl.pallas_call(
        functools.partial(atom_kernel, rows * devices),
        out_shape=(jax.ShapeDtypeStruct((rows, width), BF), tile, tile),
        in_specs=[SMEM] + [VMEM] * 11,
        out_specs=(VMEM, VMEM, VMEM),
        compiler_params=pltpu.CompilerParams(vmem_limit_bytes=40 << 20),
    )(
        window_start,
        atom_feats,
        before,
        after,
        atom_to_token.reshape(1, rows),
        atom_bias,
        token_single,
        token_mask.reshape(-1, 128),
        w_atom,
        w_atom_out,
        w_to_token,
        w_token,
    )
    dma = pltpu.SemaphoreType.DMA
    qall, kall = pl.pallas_call(
        exchange_kernel,
        out_shape=(
            jax.ShapeDtypeStruct((n_atom, n_col, toks, 128), BF),
            jax.ShapeDtypeStruct((n_atom // n_col, n_row, n_col, toks, 128), BF),
        ),
        in_specs=[VMEM] * 2,
        out_specs=(VMEM, VMEM),
        scratch_shapes=[
            dma((2, n_atom)),
            dma((n_atom,)),
            dma((n_atom,)),
            dma((2, max(n_row, n_col))),
            dma((n_col,)),
            dma((n_row,)),
        ],
        compiler_params=pltpu.CompilerParams(
            collective_id=0, has_side_effects=True, vmem_limit_bytes=40 << 20
        ),
    )(qg, kv)
    q_rows, k_cols = pair_bias.shape[1:]
    tile_rows = 256
    part = pl.pallas_call(
        attend_kernel,
        grid=(q_rows // tile_rows,),
        out_shape=jax.ShapeDtypeStruct((q_rows, 128), BF),
        in_specs=[
            pl.BlockSpec((tile_rows, 128), lambda i: (i, 0)),
            pl.BlockSpec((k_cols, 128), lambda i: (0, 0)),
            pl.BlockSpec((1, tile_rows, k_cols), lambda i: (0, i, 0)),
        ],
        out_specs=pl.BlockSpec((tile_rows, 128), lambda i: (i, 0)),
        scratch_shapes=[pltpu.VMEM((tile_rows, k_cols), F32), pltpu.VMEM((tile_rows, k_cols), BF)],
        compiler_params=pltpu.CompilerParams(vmem_limit_bytes=40 << 20),
    )(qall.reshape(q_rows, 128), kall.reshape(k_cols, 128), pair_bias)
    out_rows = q_rows // n_atom
    summed = pl.pallas_call(
        merge_kernel,
        out_shape=jax.ShapeDtypeStruct((out_rows, w_out.shape[1]), BF),
        in_specs=[VMEM] * 3,
        out_specs=VMEM,
        scratch_shapes=[
            pltpu.VMEM((n_col, q_rows // n_col, 128), BF),
            pltpu.VMEM((n_atom // n_col, HD, out_rows), BF),
            pltpu.VMEM((n_atom, HD, out_rows), BF),
            dma((n_col,)),
            dma((n_col,)),
            dma((n_atom // n_col, n_col)),
            dma((n_atom,)),
        ],
        compiler_params=pltpu.CompilerParams(
            collective_id=1, has_side_effects=True, vmem_limit_bytes=40 << 20
        ),
    )(
        part.reshape(n_col, q_rows // n_col, 128),
        qall.reshape(n_col, q_rows // n_col, 128),
        w_out.T,
    )
    return (update, summed)


def solution(mesh):
    placed = (
        P(("atom", "row", "col"), None),
        P(("atom", "row", "col")),
        P(("atom", "row", "col")),
        P(("atom", "row", "col"), None),
        P(("atom", "row", "col"), None),
        P(),
        P("atom", "row", "col"),
        P(),
        P(),
        P(),
        P(),
        P(None, "col"),
    )
    return jax.shard_map(
        shards,
        mesh=mesh,
        in_specs=placed,
        out_specs=(P(("atom", "row", "col"), None), P(("row", "atom"), "col")),
        check_vma=False,
    )
```

```python
import functools

import jax
import jax.numpy as jnp
from jax import lax
from jax.experimental import pallas as pl
from jax.experimental.pallas import tpu as pltpu
from jax.sharding import PartitionSpec as P

AH = 4
QB = 32
KW = 128
HALO = 64
HD = 48
EPS = 1e-05
NEG = -1e30
BF = jnp.bfloat16
F32 = jnp.float32
MESH = pl.DeviceIdType.MESH
VMEM = pl.BlockSpec(memory_space=pltpu.VMEM)
SMEM = pl.BlockSpec(memory_space=pltpu.SMEM)
NT = (((1,), (1,)), ((), ()))


def layer_norm(values):
    centre = values - jnp.mean(values, axis=-1, keepdims=True)
    spread = jnp.mean(centre * centre, axis=-1, keepdims=True)
    return (centre * lax.rsqrt(spread + EPS)).astype(BF)


def dot(a, b):
    return jnp.dot(a, b, preferred_element_type=F32)


def iota(shape, dim):
    return lax.broadcasted_iota(jnp.int32, shape, dim)


def place():
    return lax.axis_index("atom"), lax.axis_index("row"), lax.axis_index("col")


def atoms(all_atoms, start_ref, feats_ref, before_ref, after_ref, bias_ref, w_atom_ref, device):
    rows, width = feats_ref.shape
    feats = feats_ref[...].astype(F32)
    wide = jnp.concatenate([before_ref[...].astype(F32), feats, after_ref[...].astype(F32)], axis=0)
    proj = dot(layer_norm(wide), w_atom_ref[...])
    queries = proj[HALO : HALO + rows, :width].astype(BF)
    pairs = proj[:, width : 3 * width].astype(BF)
    gate = jax.nn.sigmoid(proj[HALO : HALO + rows, 3 * width :])
    part = width // AH
    reach = KW + QB
    lane_head = iota((QB, width), 1) // part
    ahead = iota((KW, reach), 1) - iota((KW, reach), 0)
    slot = iota((1, KW), 1)
    blocks = []
    for b in range(rows // QB):
        start = start_ref[b]
        shift = start - (device * rows + QB * b) + HALO
        pick = jnp.where(ahead == shift, 1.0, 0.0).astype(BF)
        keyed = dot(pick, pairs[QB * b : QB * b + reach]).astype(BF)
        query = queries[QB * b : QB * (b + 1)]
        stacked = jnp.concatenate(
            [jnp.where(lane_head == h, query, jnp.zeros_like(query)) for h in range(AH)], axis=0
        )
        scores = lax.dot_general(stacked, keyed[:, :width], NT, preferred_element_type=F32)
        bias = jnp.concatenate(
            [bias_ref[QB * b : QB * (b + 1), KW * h : KW * (h + 1)] for h in range(AH)], axis=0
        )
        scores = scores * part ** (-0.5) + bias.astype(F32)
        placed = start + slot
        scores = jnp.where((placed >= 0) & (placed < all_atoms), scores, NEG)
        expo = jnp.exp(scores - jnp.max(scores, axis=-1, keepdims=True))
        weights = (expo / jnp.sum(expo, axis=-1, keepdims=True)).astype(BF)
        mixed = dot(weights, keyed[:, width:])
        block = jnp.zeros((QB, width), F32)
        for h in range(AH):
            block = jnp.where(lane_head == h, mixed[QB * h : QB * (h + 1)], block)
        blocks.append(block)
    return feats, (jnp.concatenate(blocks, axis=0) * gate).astype(BF)


def tokens(member_ref, single_ref, hidden, device):
    toks, rows = single_ref.shape[0], hidden.shape[0]
    local = member_ref[...] - device * toks
    member = jnp.where(local == iota((toks, rows), 0), 1.0, 0.0)
    sums = dot(member.astype(BF), hidden)
    counts = jnp.sum(member, axis=1, keepdims=True)
    return layer_norm(single_ref[...].astype(F32) + sums / counts)


def tiles(head_data, mask_ref, qg_ref, kv_ref, device):
    heads, toks = qg_ref.shape[:2]
    span = 8 * HD
    stacked = jnp.concatenate(
        [head_data[:, span * p : span * (p + 1)] for p in range(heads // 2)], axis=0
    )
    source, target = iota((span, 512), 0), iota((span, 512), 1)
    lane = target % 128
    kind = (target // 128) % 2
    base = (target // 256) * 4 * HD + kind * HD
    first = base + lane
    second = base + jnp.where(kind == 0, 2 * HD, 0) + lane
    wanted = jnp.where(lane < HD, first, jnp.where(lane < 2 * HD, second, -1))
    spread = dot(stacked, jnp.where(source == wanted, 1.0, 0.0).astype(BF))
    live = jnp.sum(jnp.sum(mask_ref[...], axis=0, keepdims=True), axis=1, keepdims=True)
    token = device * toks + iota((toks, 128), 0)
    lanes = iota((toks, 128), 1)
    masked = jnp.where(token < live, 0.0, NEG)
    for h in range(heads):
        rows_h = slice(toks * (h // 2), toks * (h // 2 + 1))
        at = 256 * (h % 2)
        qg = jnp.where(lanes == 2 * HD, 1.0, spread[rows_h, at : at + 128])
        kv = jnp.where(lanes == 2 * HD, masked, spread[rows_h, at + 128 : at + 256])
        kv = jnp.where(lanes == 2 * HD + 1, 1.0, kv)
        qg_ref[h] = qg.astype(BF)
        kv_ref[h] = kv.astype(BF)


def attend(qg, keys_at, bias_at, score_ref, weight_ref, keys_all):
    rows, keys = score_ref.shape
    chunk = 256
    lane = iota((rows, 128), 1)
    query = jnp.where((lane < HD) | (lane == 2 * HD), qg, jnp.zeros_like(qg))
    peak = jnp.full((rows, 128), -jnp.inf, F32)
    for at in range(0, keys, chunk):
        part = lax.dot_general(query, keys_at(at, chunk), NT, preferred_element_type=F32)
        part = part * HD ** (-0.5) + bias_at(at, chunk).astype(F32)
        score_ref[:, at : at + chunk] = part
        for k in range(0, chunk, 128):
            peak = jnp.maximum(peak, part[:, k : k + 128])
    top = jnp.max(peak, axis=1, keepdims=True)
    for at in range(0, keys, chunk):
        weight_ref[:, at : at + chunk] = jnp.exp(score_ref[:, at : at + chunk] - top).astype(BF)
    mixed = dot(weight_ref[...], keys_all())
    total = mixed[:, 2 * HD + 1 : 2 * HD + 2]
    high = top.astype(BF).astype(F32)
    middle = (top - high).astype(BF).astype(F32)
    low = top - high - middle
    total_high = total.astype(BF).astype(F32)
    result = mixed
    for at, value in enumerate((high, middle, low, total_high, total - total_high)):
        result = jnp.where(lane == at, value, result)
    return result.astype(BF)


def merged(parts, gates):
    parts = [p.astype(F32) for p in parts]
    tops = [p[:, 0:1] + p[:, 1:2] + p[:, 2:3] for p in parts]
    totals = [p[:, 3:4] + p[:, 4:5] for p in parts]
    top = functools.reduce(jnp.maximum, tops)
    scales = [jnp.exp(t - top) for t in tops]
    total = sum(s * t for s, t in zip(scales, totals))
    mixed = sum(s * p for s, p in zip(scales, parts))
    attended = jnp.transpose(mixed / total * jax.nn.sigmoid(gates.astype(F32)))
    return attended[HD : 2 * HD].astype(BF)


def unless(own, remote, local):
    @pl.when(jnp.logical_not(own))
    def _():
        remote()

    @pl.when(own)
    def _():
        local()


def whole_kernel(
    all_atoms,
    start_ref,
    feats_in,
    before_in,
    after_in,
    w_atom_in,
    bias_in,
    w_atom_out_in,
    w_to_token_in,
    member_in,
    single_in,
    w_token_in,
    mask_in,
    pair_in,
    w_out_in,
    update_ref,
    out_ref,
    feats_ref,
    before_ref,
    after_ref,
    w_atom_ref,
    bias_ref,
    w_atom_out_ref,
    w_to_token_ref,
    member_ref,
    single_ref,
    w_token_ref,
    mask_ref,
    pair_ref,
    w_out_ref,
    qg_ref,
    kv_ref,
    qall_ref,
    kall_ref,
    score_ref,
    weight_ref,
    part_ref,
    got_ref,
    head_ref,
    all_ref,
    load,
    send,
    q_sem,
    k_sem,
    g_send,
    gq_sem,
    gk_sem,
    m_send,
    m_recv,
    h_send,
    h_recv,
):
    a, r, c = place()
    n_atom, n_row, n_col = (lax.axis_size(x) for x in ("atom", "row", "col"))
    group_q, group_k = n_atom // n_row, n_atom // n_col
    device = (a * n_row + r) * n_col + c
    barrier = pltpu.get_barrier_semaphore()
    loads = [
        pltpu.make_async_copy(source, target, load.at[i])
        for i, (source, target) in enumerate(
            (
                (feats_in, feats_ref),
                (before_in, before_ref),
                (after_in, after_ref),
                (w_atom_in, w_atom_ref),
                (bias_in, bias_ref),
                (w_atom_out_in, w_atom_out_ref),
                (w_to_token_in, w_to_token_ref),
                (member_in, member_ref),
                (single_in, single_ref),
                (w_token_in, w_token_ref),
                (mask_in, mask_ref),
                (pair_in, pair_ref),
                (w_out_in, w_out_ref),
            )
        )
    ]
    for copy in loads:
        copy.start()

    def signal(to):
        pl.semaphore_signal(barrier, inc=1, device_id=to, device_id_type=MESH)

    own_q = a // group_q == r
    own_k = a // group_k == c

    def greet(i, carry):
        source_k = (group_k * c + i // n_col, r, i % n_col)

        @pl.when(jnp.logical_not(own_k & (source_k[0] == a) & (source_k[2] == c)))
        def _():
            signal(source_k)

        source_q = (group_q * r + i // n_row, i % n_row, c)

        @pl.when(jnp.logical_not(own_q & (source_q[0] == a) & (source_q[1] == r)))
        def _():
            signal(source_q)

        @pl.when(jnp.logical_not(own_k & (i == a)))
        def _():
            signal((i, r, a // group_k))

        return carry

    lax.fori_loop(0, n_atom, greet, 0)
    for step in range(1, n_col):
        signal((a, r, lax.rem(c + step, n_col)))
    for step in range(1, n_row):
        signal((a, lax.rem(r + step, n_row), c))

    for copy in loads[:5]:
        copy.wait()
    feats, gated = atoms(
        all_atoms, start_ref, feats_ref, before_ref, after_ref, bias_ref, w_atom_ref, device
    )
    for copy in loads[5:9]:
        copy.wait()
    change = dot(gated, w_atom_out_ref[...])
    update_ref[...] = change.astype(BF)
    hidden = jnp.maximum(dot((feats + change).astype(BF), w_to_token_ref[...]), 0.0).astype(BF)
    normed = tokens(member_ref, single_ref, hidden, device)
    for copy in loads[9:11]:
        copy.wait()
    head_data = dot(normed, w_token_ref[...]).astype(BF)
    tiles(head_data, mask_ref, qg_ref, kv_ref, device)

    count = 3 * n_atom + (n_col - 1) + (n_row - 1)
    pl.semaphore_wait(barrier, count - own_q.astype(jnp.int32) - 2 * own_k.astype(jnp.int32))

    q_slot = lax.rem(a, group_q) * n_row + r
    k_four = lax.rem(a, group_k)
    k_slot = k_four * n_col + c

    def q_copy(to):
        return pltpu.make_async_remote_copy(
            src_ref=qg_ref.at[to],
            dst_ref=qall_ref.at[q_slot, c],
            send_sem=send.at[0, to],
            recv_sem=q_sem.at[q_slot],
            device_id=(to, a // group_q, c),
            device_id_type=MESH,
        )

    def k_copy(to):
        return pltpu.make_async_remote_copy(
            src_ref=kv_ref.at[to],
            dst_ref=kall_ref.at[k_four, r, c],
            send_sem=send.at[1, to],
            recv_sem=k_sem.at[k_slot],
            device_id=(to, r, a // group_k),
            device_id_type=MESH,
        )

    def start(i, carry):
        half = n_atom // 2
        to = lax.rem(a // half + 1 + i // half, 2) * half + lax.rem(a + i, half)
        unless(
            own_k & (to == a),
            lambda: k_copy(to).start(),
            lambda: pltpu.make_async_copy(
                kv_ref.at[to], kall_ref.at[k_four, r, c], k_sem.at[k_slot]
            ).start(),
        )
        unless(
            own_q & (to == a),
            lambda: q_copy(to).start(),
            lambda: pltpu.make_async_copy(
                qg_ref.at[to], qall_ref.at[q_slot, c], q_sem.at[q_slot]
            ).start(),
        )
        return carry

    lax.fori_loop(0, n_atom, start, 0)

    def arrive_k(i, carry):
        pltpu.make_async_copy(
            kv_ref.at[0], kall_ref.at[i // n_col, r, i % n_col], k_sem.at[i]
        ).wait()
        return carry

    def arrive_q(i, carry):
        pltpu.make_async_copy(qg_ref.at[0], qall_ref.at[i, c], q_sem.at[i]).wait()
        return carry

    def gather_q(step):
        mine = qall_ref.at[:, c]
        return pltpu.make_async_remote_copy(
            src_ref=mine,
            dst_ref=mine,
            send_sem=g_send.at[0, step],
            recv_sem=gq_sem.at[step],
            device_id=(a, r, lax.rem(c + step, n_col)),
            device_id_type=MESH,
        )

    def gather_k(step):
        mine = kall_ref.at[:, r]
        return pltpu.make_async_remote_copy(
            src_ref=mine,
            dst_ref=mine,
            send_sem=g_send.at[1, step],
            recv_sem=gk_sem.at[step],
            device_id=(a, lax.rem(r + step, n_row), c),
            device_id_type=MESH,
        )

    lax.fori_loop(0, n_atom, arrive_k, 0)
    for step in range(1, n_row):
        gather_k(step).start()
    lax.fori_loop(0, n_atom, arrive_q, 0)
    for step in range(1, n_col):
        gather_q(step).start()
    for step in range(1, n_col):
        gather_q(step).wait_recv()
    for step in range(1, n_row):
        gather_k(step).wait_recv()
    for copy in loads[11:]:
        copy.wait()

    tile_rows, keys = score_ref.shape
    q_rows = pair_ref.shape[1]
    per_slot = q_rows // n_atom
    per_tile = tile_rows // per_slot
    per_chunk = q_rows // n_col // tile_rows

    def keys_at(at, chunk):
        slots = chunk // per_slot
        index = at // per_slot
        block = kall_ref[index // n_row, index % n_row : index % n_row + slots]
        return block.reshape(chunk, 128)

    def partial(step):
        to = lax.rem(c + step, n_col)
        return pltpu.make_async_remote_copy(
            src_ref=part_ref.at[to],
            dst_ref=got_ref.at[step],
            send_sem=m_send.at[step],
            recv_sem=m_recv.at[step],
            device_id=(a, r, to),
            device_id_type=MESH,
        )

    def one_tile(i, carry):
        step = i // per_chunk + 1
        to = lax.rem(c + step, n_col)
        inner = lax.rem(i, per_chunk)
        index = to * per_chunk + inner
        span = pl.ds(pl.multiple_of(index * tile_rows, tile_rows), tile_rows)
        part_ref[to, pl.ds(pl.multiple_of(inner * tile_rows, tile_rows), tile_rows)] = attend(
            qall_ref[pl.ds(index * per_tile, per_tile)].reshape(tile_rows, 128),
            keys_at,
            lambda at, chunk: pair_ref[0, span, at : at + chunk],
            score_ref,
            weight_ref,
            lambda: kall_ref[...].reshape(keys, 128),
        )

        @pl.when((inner == per_chunk - 1) & (step < n_col))
        def _():
            partial(step).start()

        return carry

    lax.fori_loop(0, n_col * per_chunk, one_tile, 0)
    for step in range(1, n_col):
        partial(step).wait_recv()

    def head_copy(j, k):
        return pltpu.make_async_remote_copy(
            src_ref=head_ref.at[j],
            dst_ref=all_ref.at[a],
            send_sem=h_send.at[j, k],
            recv_sem=h_recv.at[a],
            device_id=(group_k * c + j, r, lax.rem(c + k, n_col)),
            device_id_type=MESH,
        )

    rows = head_ref.shape[2]

    def one_head(j, carry):
        span = pl.ds(pl.multiple_of(j * rows, rows), rows)
        gates = qall_ref[c * group_k + j].reshape(rows, 128)
        parts = [part_ref[c, span]] + [got_ref[step, span] for step in range(1, n_col)]
        head_ref[j] = merged(parts, gates)
        for k in range(1, n_col):
            head_copy(j, k).start()
        unless(
            own_k & (group_k * c + j == a),
            lambda: head_copy(j, 0).start(),
            lambda: pltpu.make_async_copy(head_ref.at[j], all_ref.at[a], h_recv.at[a]).start(),
        )
        return carry

    lax.fori_loop(0, group_k, one_head, 0)

    def arrive(i, carry):
        pltpu.make_async_copy(head_ref.at[0], all_ref.at[i], h_recv.at[i]).wait()
        return carry

    lax.fori_loop(0, n_atom, arrive, 0)
    heads = all_ref[...].reshape(n_atom * HD, rows)
    out_ref[...] = jnp.transpose(dot(w_out_ref[...], heads)).astype(BF)

    def sent(to, carry):
        @pl.when(jnp.logical_not(own_q & (to == a)))
        def _():
            q_copy(to).wait_send()

        @pl.when(jnp.logical_not(own_k & (to == a)))
        def _():
            k_copy(to).wait_send()

        return carry

    lax.fori_loop(0, n_atom, sent, 0)
    for step in range(1, n_col):
        gather_q(step).wait_send()
        partial(step).wait_send()
    for step in range(1, n_row):
        gather_k(step).wait_send()

    def head_sent(j, carry):
        for k in range(1, n_col):
            head_copy(j, k).wait_send()

        @pl.when(jnp.logical_not(own_k & (group_k * c + j == a)))
        def _():
            head_copy(j, 0).wait_send()

        return carry

    lax.fori_loop(0, group_k, head_sent, 0)


def shards(
    atom_feats,
    atom_to_token,
    window_start,
    atom_bias,
    token_single,
    token_mask,
    pair_bias,
    w_atom,
    w_atom_out,
    w_to_token,
    w_token,
    w_out,
):
    rows, width = atom_feats.shape
    toks = token_single.shape[0]
    axes = ("atom", "row", "col")
    n_atom, n_row, n_col = (lax.axis_size(x) for x in axes)
    devices = n_atom * n_row * n_col
    up = [(i, (i + 1) % devices) for i in range(devices)]
    down = [(j, i) for i, j in up]
    before = lax.ppermute(atom_feats[rows - HALO :], axes, up)
    after = lax.ppermute(atom_feats[:HALO], axes, down)
    q_rows, k_cols = pair_bias.shape[1:]
    out_rows = q_rows // n_atom
    group = n_atom // n_col
    tile_rows = 256
    operands = (
        atom_feats,
        before,
        after,
        w_atom,
        atom_bias,
        w_atom_out,
        w_to_token,
        atom_to_token.reshape(1, rows),
        token_single,
        w_token,
        token_mask.reshape(-1, 128),
        pair_bias,
        w_out.T,
    )
    dma = pltpu.SemaphoreType.DMA
    return pl.pallas_call(
        functools.partial(whole_kernel, rows * devices),
        out_shape=(
            jax.ShapeDtypeStruct((rows, width), BF),
            jax.ShapeDtypeStruct((out_rows, w_out.shape[1]), BF),
        ),
        in_specs=[SMEM] + [pl.BlockSpec(memory_space=pl.ANY)] * len(operands),
        out_specs=(VMEM, VMEM),
        scratch_shapes=[pltpu.VMEM(x.shape, x.dtype) for x in operands]
        + [
            pltpu.VMEM((n_atom, toks, 128), BF),
            pltpu.VMEM((n_atom, toks, 128), BF),
            pltpu.VMEM((n_atom, n_col, toks, 128), BF),
            pltpu.VMEM((group, n_row, n_col, toks, 128), BF),
            pltpu.VMEM((tile_rows, k_cols), F32),
            pltpu.VMEM((tile_rows, k_cols), BF),
            pltpu.VMEM((n_col, q_rows // n_col, 128), BF),
            pltpu.VMEM((n_col, q_rows // n_col, 128), BF),
            pltpu.VMEM((group, HD, out_rows), BF),
            pltpu.VMEM((n_atom, HD, out_rows), BF),
            dma((len(operands),)),
            dma((2, n_atom)),
            dma((n_atom,)),
            dma((n_atom,)),
            dma((2, max(n_row, n_col))),
            dma((n_col,)),
            dma((n_row,)),
            dma((n_col,)),
            dma((n_col,)),
            dma((group, n_col)),
            dma((n_atom,)),
        ],
        compiler_params=pltpu.CompilerParams(
            collective_id=0, has_side_effects=True, vmem_limit_bytes=56 << 20
        ),
    )(window_start, *operands)


def solution(mesh):
    placed = (
        P(("atom", "row", "col"), None),
        P(("atom", "row", "col")),
        P(("atom", "row", "col")),
        P(("atom", "row", "col"), None),
        P(("atom", "row", "col"), None),
        P(),
        P("atom", "row", "col"),
        P(),
        P(),
        P(),
        P(),
        P(None, "col"),
    )
    return jax.shard_map(
        shards,
        mesh=mesh,
        in_specs=placed,
        out_specs=(P(("atom", "row", "col"), None), P(("row", "atom"), "col")),
        check_vma=False,
    )
```

```python
import functools

import jax
import jax.numpy as jnp
from jax import lax
from jax.experimental import pallas as pl
from jax.experimental.pallas import tpu as pltpu
from jax.sharding import PartitionSpec as P

AH = 4
QB = 32
KW = 128
HALO = 64
HD = 48
EPS = 1e-05
NEG = -1e30
BF = jnp.bfloat16
F32 = jnp.float32
MESH = pl.DeviceIdType.MESH
VMEM = pl.BlockSpec(memory_space=pltpu.VMEM)
SMEM = pl.BlockSpec(memory_space=pltpu.SMEM)
NT = (((1,), (1,)), ((), ()))


def layer_norm(values):
    centre = values - jnp.mean(values, axis=-1, keepdims=True)
    spread = jnp.mean(centre * centre, axis=-1, keepdims=True)
    return (centre * lax.rsqrt(spread + EPS)).astype(BF)


def dot(a, b):
    return jnp.dot(a, b, preferred_element_type=F32)


def iota(shape, dim):
    return lax.broadcasted_iota(jnp.int32, shape, dim)


def place():
    return lax.axis_index("atom"), lax.axis_index("row"), lax.axis_index("col")


def project(feats, w_atom_ref, first, last):
    return dot(layer_norm(feats.astype(F32)), w_atom_ref[:, first:last])


def window(b, all_atoms, first_atom, start, query, pairs, bias_ref):
    width = query.shape[1]
    part = width // AH
    lane_head = iota((QB, width), 1) // part
    shift = start - (first_atom + QB * b) + HALO
    reach = pairs.shape[0]
    ahead = iota((KW, reach), 1) - iota((KW, reach), 0)
    pick = jnp.where(ahead == shift, 1.0, 0.0).astype(BF)
    keyed = dot(pick, pairs).astype(BF)
    stacked = jnp.concatenate(
        [jnp.where(lane_head == h, query, jnp.zeros_like(query)) for h in range(AH)], axis=0
    )
    scores = lax.dot_general(stacked, keyed[:, :width], NT, preferred_element_type=F32)
    bias = jnp.concatenate(
        [bias_ref[QB * b : QB * (b + 1), KW * h : KW * (h + 1)] for h in range(AH)], axis=0
    )
    scores = scores * part ** (-0.5) + bias.astype(F32)
    placed = start + iota((1, KW), 1)
    scores = jnp.where((placed >= 0) & (placed < all_atoms), scores, NEG)
    expo = jnp.exp(scores - jnp.max(scores, axis=-1, keepdims=True))
    weights = (expo / jnp.sum(expo, axis=-1, keepdims=True)).astype(BF)
    mixed = dot(weights, keyed[:, width:])
    block = mixed[:QB]
    for h in range(1, AH):
        block = jnp.where(lane_head == h, mixed[QB * h : QB * (h + 1)], block)
    return block


def tokens(member_ref, single_ref, hidden, device):
    toks, rows = single_ref.shape[0], hidden.shape[0]
    local = member_ref[...] - device * toks
    member = jnp.where(local == iota((toks, rows), 0), 1.0, 0.0)
    sums = dot(member.astype(BF), hidden)
    counts = jnp.sum(member, axis=1, keepdims=True)
    return layer_norm(single_ref[...].astype(F32) + sums / counts)


def tiles(head_data, mask_ref, qg_ref, kv_ref, device):
    heads, toks = qg_ref.shape[:2]
    span = 8 * HD
    stacked = jnp.concatenate(
        [head_data[:, span * p : span * (p + 1)] for p in range(heads // 2)], axis=0
    )
    source, target = iota((span, 512), 0), iota((span, 512), 1)
    lane = target % 128
    kind = (target // 128) % 2
    base = (target // 256) * 4 * HD
    first = base + jnp.where(kind == 0, 3 * HD, 2 * HD) + lane
    second = base + jnp.where(kind == 0, 0, HD) + lane - HD
    wanted = jnp.where(lane < HD, first, jnp.where(lane < 2 * HD, second, -1))
    spread = dot(stacked, jnp.where(source == wanted, 1.0, 0.0).astype(BF))
    live = jnp.sum(jnp.sum(mask_ref[...], axis=0, keepdims=True), axis=1, keepdims=True)
    token = device * toks + iota((toks, 128), 0)
    lanes = iota((toks, 128), 1)
    masked = jnp.where(token < live, 0.0, NEG)
    for h in range(heads):
        rows_h = slice(toks * (h // 2), toks * (h // 2 + 1))
        at = 256 * (h % 2)
        qg = jnp.where(lanes == 2 * HD, 1.0, spread[rows_h, at : at + 128])
        kv = jnp.where(lanes == 2 * HD, masked, spread[rows_h, at + 128 : at + 256])
        kv = jnp.where(lanes == 2 * HD + 1, 1.0, kv)
        qg_ref[h] = qg.astype(BF)
        kv_ref[h] = kv.astype(BF)


def summary(mixed, top):
    lane = iota(mixed.shape, 1)
    total = mixed[:, 2 * HD + 1 : 2 * HD + 2]
    high = top.astype(BF).astype(F32)
    middle = (top - high).astype(BF).astype(F32)
    total_high = total.astype(BF).astype(F32)
    for at, value in enumerate((high, middle, top - high - middle, total_high, total - total_high)):
        mixed = jnp.where(lane == HD + at, value, mixed)
    return mixed


def paired(first, second):
    return jnp.where(iota(first.shape, 1) < 64, first, pltpu.roll(second, 64, 1))


def merged(parts, gates):
    parts = [p.astype(F32) for p in parts]
    scales, totals = [], []
    for at in (HD, 64 + HD):
        tops = [p[:, at : at + 1] + p[:, at + 1 : at + 2] + p[:, at + 2 : at + 3] for p in parts]
        counts = [p[:, at + 3 : at + 4] + p[:, at + 4 : at + 5] for p in parts]
        top = functools.reduce(jnp.maximum, tops)
        scales.append([jnp.exp(t - top) for t in tops])
        totals.append(sum(s * t for s, t in zip(scales[-1], counts)))
    low = iota(parts[0].shape, 1) < 64
    mixed = sum(jnp.where(low, s, t) * p for s, t, p in zip(*scales, parts))
    attended = mixed / jnp.where(low, *totals) * jax.nn.sigmoid(gates)
    return jnp.transpose(attended).astype(BF)


def unless(own, remote, local):
    @pl.when(jnp.logical_not(own))
    def _():
        remote()

    @pl.when(own)
    def _():
        local()


def whole_kernel(
    all_atoms,
    start_ref,
    feats_in,
    w_atom_in,
    bias_in,
    w_atom_out_in,
    w_to_token_in,
    member_in,
    single_in,
    w_token_in,
    mask_in,
    pair_in,
    w_out_in,
    out_ref,
    feats_ref,
    w_atom_ref,
    bias_ref,
    w_atom_out_ref,
    w_to_token_ref,
    member_ref,
    single_ref,
    w_token_ref,
    mask_ref,
    pair_ref,
    w_out_ref,
    halo_ref,
    mixed_ref,
    qg_ref,
    kv_ref,
    qall_ref,
    kall_ref,
    query_ref,
    peak_ref,
    score_ref,
    weight_ref,
    part_ref,
    got_ref,
    head_ref,
    all_ref,
    load,
    halo_send,
    halo_recv,
    send,
    q_sem,
    k_sem,
    g_send,
    gq_sem,
    gk_sem,
    m_send,
    m_recv,
    h_send,
    h_recv,
):
    a, r, c = place()
    n_atom, n_row, n_col = (lax.axis_size(x) for x in ("atom", "row", "col"))
    group_q, group_k = n_atom // n_row, n_atom // n_col
    devices = n_atom * n_row * n_col
    device = (a * n_row + r) * n_col + c
    rows = feats_ref.shape[0]
    barrier = pltpu.get_barrier_semaphore()
    loads = [
        pltpu.make_async_copy(source, target, load.at[i])
        for i, (source, target) in enumerate(
            (
                (feats_in, feats_ref),
                (w_atom_in, w_atom_ref),
                (bias_in, bias_ref),
                (w_atom_out_in, w_atom_out_ref),
                (w_to_token_in, w_to_token_ref),
                (member_in, member_ref),
                (single_in, single_ref),
                (w_token_in, w_token_ref),
                (mask_in, mask_ref),
                (pair_in, pair_ref),
                (w_out_in, w_out_ref),
            )
        )
    ]
    for copy in loads:
        copy.start()

    def signal(to):
        pl.semaphore_signal(barrier, inc=1, device_id=to, device_id_type=MESH)

    own_q = a // group_q == r
    own_k = a // group_k == c
    own_h = lax.rem(a, n_row) == c

    def greet(i, carry):
        source_k = (group_k * c + i // n_col, r, i % n_col)

        @pl.when(jnp.logical_not(own_k & (source_k[0] == a) & (source_k[2] == c)))
        def _():
            signal(source_k)

        source_q = (group_q * r + i // n_row, i % n_row, c)

        @pl.when(jnp.logical_not(own_q & (source_q[0] == a) & (source_q[1] == r)))
        def _():
            signal(source_q)

        @pl.when(jnp.logical_not(own_h & (i == a)))
        def _():
            signal((i, r, lax.rem(a, n_row)))

        return carry

    lax.fori_loop(0, n_atom, greet, 0)
    for step in range(1, n_col):
        signal((a, r, lax.rem(c + step, n_col)))
    for step in range(1, n_row):
        signal((a, lax.rem(r + step, n_row), c))
    for step in (1, devices - 1):
        other = lax.rem(device + step, devices)
        signal((other // (n_row * n_col), lax.rem(other // n_col, n_row), lax.rem(other, n_col)))

    def halo_copy(side):
        other = lax.rem(device + (1 if side == 0 else devices - 1), devices)
        edge = rows - HALO if side == 0 else 0
        return pltpu.make_async_remote_copy(
            src_ref=feats_in.at[pl.ds(edge, HALO)],
            dst_ref=halo_ref.at[side],
            send_sem=halo_send.at[side],
            recv_sem=halo_recv.at[side],
            device_id=(
                other // (n_row * n_col),
                lax.rem(other // n_col, n_row),
                lax.rem(other, n_col),
            ),
            device_id_type=MESH,
        )

    def drain_halo():
        for side in range(2):
            halo_copy(side).wait_send()

    for copy in loads[:3]:
        copy.wait()
    rows, width = feats_ref.shape
    first_atom = device * rows
    with jax.named_scope("inner_windows"):
        feats = feats_ref[...]
        proj = project(feats, w_atom_ref, 0, 4 * width)
        queries = proj[:, :width].astype(BF)
        pairs = proj[:, width : 3 * width].astype(BF)
        gate = jax.nn.sigmoid(proj[:, 3 * width :])
        edge = HALO // QB
        blocks = rows // QB
        inner = range(edge, blocks - edge)

        def one_window(b, reach):
            query = queries[QB * b : QB * (b + 1)]
            mixed_ref[QB * b : QB * (b + 1)] = window(
                b, all_atoms, first_atom, start_ref[b], query, reach, bias_ref
            )

        for b in inner:
            one_window(b, pairs[QB * (b - edge) : QB * (b + edge + 1)])
    with jax.named_scope("barrier"):
        count = 3 * n_atom + (n_col - 1) + (n_row - 1) + 2
        for own in (own_q, own_k, own_h):
            count = count - own.astype(jnp.int32)
        pl.semaphore_wait(barrier, count)
    with jax.named_scope("halo"):
        for side in range(2):
            halo_copy(side).start()
        for side in range(2):
            halo_copy(side).wait_recv()
    with jax.named_scope("outer_windows"):
        around = project(halo_ref[...].reshape(2 * HALO, width), w_atom_ref, width, 3 * width)
        around = around.astype(BF)
        before, after = around[:HALO], around[HALO:]
        wide = jnp.concatenate([before, pairs[: QB * 2 * edge]], axis=0)
        for b in range(edge):
            one_window(b, wide[QB * b : QB * (b + 2 * edge + 1)])
        wide = jnp.concatenate([pairs[rows - QB * 2 * edge :], after], axis=0)
        for b in range(edge):
            one_window(blocks - edge + b, wide[QB * b : QB * (b + 2 * edge + 1)])
        gated = (mixed_ref[...] * gate).astype(BF)
    with jax.named_scope("tokens"):
        for copy in loads[3:7]:
            copy.wait()
        change = dot(gated, w_atom_out_ref[...])
        out_ref[:rows] = change.astype(BF)
        acted = (feats.astype(F32) + change).astype(BF)
        hidden = jnp.maximum(dot(acted, w_to_token_ref[...]), 0.0).astype(BF)
        normed = tokens(member_ref, single_ref, hidden, device)
        for copy in loads[7:9]:
            copy.wait()
        head_data = dot(normed, w_token_ref[...]).astype(BF)
        tiles(head_data, mask_ref, qg_ref, kv_ref, device)

    q_slot = lax.rem(a, group_q) * n_row + r
    k_four = lax.rem(a, group_k)
    k_slot = k_four * n_col + c

    def q_copy(to):
        return pltpu.make_async_remote_copy(
            src_ref=qg_ref.at[to],
            dst_ref=qall_ref.at[q_slot, c],
            send_sem=send.at[0, to],
            recv_sem=q_sem.at[q_slot],
            device_id=(to, a // group_q, c),
            device_id_type=MESH,
        )

    def k_copy(to):
        return pltpu.make_async_remote_copy(
            src_ref=kv_ref.at[to],
            dst_ref=kall_ref.at[r, k_four, c],
            send_sem=send.at[1, to],
            recv_sem=k_sem.at[k_slot],
            device_id=(to, r, a // group_k),
            device_id_type=MESH,
        )

    def drain_tiles():
        def sent(to, carry):
            unless(own_q & (to == a), lambda: q_copy(to).wait_send(), lambda: None)
            unless(own_k & (to == a), lambda: k_copy(to).wait_send(), lambda: None)
            return carry

        lax.fori_loop(0, n_atom, sent, 0)

    def start(i, carry):
        half = n_atom // 2
        to = lax.rem(a // half + 1 + i // half, 2) * half + lax.rem(a + i, half)
        unless(
            own_k & (to == a),
            lambda: k_copy(to).start(),
            lambda: pltpu.make_async_copy(
                kv_ref.at[to], kall_ref.at[r, k_four, c], k_sem.at[k_slot]
            ).start(),
        )
        unless(
            own_q & (to == a),
            lambda: q_copy(to).start(),
            lambda: pltpu.make_async_copy(
                qg_ref.at[to], qall_ref.at[q_slot, c], q_sem.at[q_slot]
            ).start(),
        )
        return carry

    with jax.named_scope("send_tiles"):
        lax.fori_loop(0, n_atom, start, 0)

    def arrive_k(i, carry):
        pltpu.make_async_copy(
            kv_ref.at[0], kall_ref.at[r, i // n_col, i % n_col], k_sem.at[i]
        ).wait()
        return carry

    def arrive_q(i, carry):
        pltpu.make_async_copy(qg_ref.at[0], qall_ref.at[i, c], q_sem.at[i]).wait()
        return carry

    def gather_q(step):
        mine = qall_ref.at[:, c]
        return pltpu.make_async_remote_copy(
            src_ref=mine,
            dst_ref=mine,
            send_sem=g_send.at[0, step],
            recv_sem=gq_sem.at[step],
            device_id=(a, r, lax.rem(c + step, n_col)),
            device_id_type=MESH,
        )

    def partner(step):
        half = n_row // 2
        return lax.rem(r // 2 + step // 2, half) * 2 + lax.rem(lax.rem(r, 2) + step % 2, 2)

    def gather_k(step):
        return pltpu.make_async_remote_copy(
            src_ref=kall_ref.at[r],
            dst_ref=kall_ref.at[r],
            send_sem=g_send.at[1, step],
            recv_sem=gk_sem.at[step],
            device_id=(a, partner(step), c),
            device_id_type=MESH,
        )

    def drain_gather():
        for step in range(1, n_col):
            gather_q(step).wait_send()
        for step in range(1, n_row):
            gather_k(step).wait_send()

    with jax.named_scope("tiles_arrive"):
        lax.fori_loop(0, n_atom, arrive_q, 0)
        for step in range(1, n_col):
            gather_q(step).start()
        lax.fori_loop(0, n_atom, arrive_k, 0)
        for step in range(1, n_row):
            gather_k(step).start()
    for copy in loads[9:]:
        copy.wait()
    with jax.named_scope("gather_q"):
        for step in range(1, n_col):
            gather_q(step).wait_recv()
    q_rows, keys = pair_ref.shape[1:]
    per_slot = q_rows // n_atom
    per_row = keys // n_row
    lane = iota((q_rows, 128), 1)
    queries = qall_ref[...].reshape(q_rows, 128)
    query_ref[...] = jnp.where(
        (lane >= HD) & (lane <= 2 * HD), queries, jnp.zeros_like(queries)
    )
    peak_ref[...] = jnp.full_like(peak_ref, -jnp.inf)

    def score(step, carry):
        source = partner(step)

        @pl.when(step > 0)
        def _():
            mine = kall_ref.at[source]
            pltpu.make_async_copy(mine, mine, gk_sem.at[step]).wait()

        held = kall_ref[source].reshape(per_row, 128)
        half = q_rows // 2
        span = half // (n_row * per_slot)
        for i in range(2):
            rows = slice(half * i, half * (i + 1))
            fours = slice(span * i, span * (i + 1))
            peak = peak_ref[fours]
            for at in range(0, per_row, 256):
                part = lax.dot_general(
                    query_ref[rows], held[at : at + 256], NT, preferred_element_type=F32
                )
                for k in range(0, 256, 128):
                    four = (at + k) // 128
                    column = four * per_row + source * 128
                    bias = pair_ref[0, rows, pl.ds(pl.multiple_of(column, 128), 128)]
                    value = part[:, k : k + 128] * HD ** (-0.5) + bias.astype(F32)
                    value = value.reshape(peak.shape)
                    column = source * per_row + at + k
                    score_ref[fours, :, :, pl.ds(pl.multiple_of(column, 128), 128)] = value
                    peak = jnp.maximum(peak, value)
            peak_ref[fours] = peak
        return carry

    with jax.named_scope("scores"):
        lax.fori_loop(0, n_row, score, 0)

    def partial(step):
        to = lax.rem(c + step, n_col)
        return pltpu.make_async_remote_copy(
            src_ref=part_ref.at[to],
            dst_ref=got_ref.at[step],
            send_sem=m_send.at[step],
            recv_sem=m_recv.at[step],
            device_id=(a, r, to),
            device_id_type=MESH,
        )

    def drain_partials():
        for step in range(1, n_col):
            partial(step).wait_send()

    def quarter(i, carry):
        to = lax.rem(c + i + 1, n_col)
        results = []
        for h in range(2):
            fours = slice(2 * h, 2 * h + 2)
            top = jnp.max(peak_ref[fours, to].reshape(2 * per_slot, 128), axis=1, keepdims=True)
            for at in range(0, keys, 256):
                part = score_ref[fours, to, :, at : at + 256].reshape(2 * per_slot, 256)
                weight_ref[h, :, at : at + 256] = jnp.exp(part - top).astype(BF)
            mixed = dot(weight_ref[h], kall_ref[...].reshape(keys, 128))
            results.append(summary(mixed, top))
        part_ref[to] = paired(*results).astype(BF)

        @pl.when(i < n_col - 1)
        def _():
            partial(i + 1).start()

        return carry

    with jax.named_scope("attention"):
        lax.fori_loop(0, n_col, quarter, 0)
    with jax.named_scope("partials_arrive"):
        for step in range(1, n_col):
            partial(step).wait_recv()

    def head_copy(j, k):
        return pltpu.make_async_remote_copy(
            src_ref=head_ref.at[j],
            dst_ref=all_ref.at[a],
            send_sem=h_send.at[j, k],
            recv_sem=h_recv.at[a],
            device_id=(n_row * j + c, r, lax.rem(c + k, n_col)),
            device_id_type=MESH,
        )

    def drain_heads():
        def sent(j, carry):
            for k in range(1, n_col):
                head_copy(j, k).wait_send()
            unless(
                own_h & (n_row * j + c == a),
                lambda: head_copy(j, 0).wait_send(),
                lambda: None,
            )
            return carry

        lax.fori_loop(0, group_k, sent, 0)

    out_rows = head_ref.shape[2]

    def one_head(j, carry):
        for k in range(1, n_col):
            head_copy(j, k).start()
        unless(
            own_h & (n_row * j + c == a),
            lambda: head_copy(j, 0).start(),
            lambda: pltpu.make_async_copy(head_ref.at[j], all_ref.at[a], h_recv.at[a]).start(),
        )
        return carry

    with jax.named_scope("merge"):
        parts = [part_ref[c]] + [got_ref[step] for step in range(1, n_col)]
        gates = [
            jnp.concatenate(
                [qall_ref[n_row * u + c].reshape(per_slot, 128) for u in (2 * h, 2 * h + 1)], axis=0
            ).astype(F32)
            for h in range(2)
        ]
        attended = merged(parts, paired(*gates))
        for u in range(group_k):
            at = 64 * (u // 2)
            head_ref[u] = attended[at : at + HD, out_rows * (u % 2) : out_rows * (u % 2 + 1)]
    with jax.named_scope("send_heads"):
        lax.fori_loop(0, group_k, one_head, 0)

    def arrive(i, carry):
        pltpu.make_async_copy(head_ref.at[0], all_ref.at[i], h_recv.at[i]).wait()
        return carry

    with jax.named_scope("heads_arrive"):
        lax.fori_loop(0, n_atom, arrive, 0)
    with jax.named_scope("output"):
        heads = all_ref[...].reshape(n_atom * HD, head_ref.shape[2])
        out_ref[rows:] = dot(w_out_ref[...], heads).astype(BF)

    drain_halo()
    drain_tiles()
    drain_gather()
    drain_partials()
    drain_heads()


def shards(
    atom_feats,
    atom_to_token,
    window_start,
    atom_bias,
    token_single,
    token_mask,
    pair_bias,
    w_atom,
    w_atom_out,
    w_to_token,
    w_token,
    w_out,
):
    rows, width = atom_feats.shape
    toks = token_single.shape[0]
    axes = ("atom", "row", "col")
    n_atom, n_row, n_col = (lax.axis_size(x) for x in axes)
    devices = n_atom * n_row * n_col
    q_rows, k_cols = pair_bias.shape[1:]
    out_rows = q_rows // n_atom
    group = n_atom // n_col
    tile_rows = q_rows // n_col // 2
    operands = (
        atom_feats,
        w_atom,
        atom_bias,
        w_atom_out,
        w_to_token,
        atom_to_token.reshape(1, rows),
        token_single,
        w_token,
        token_mask.reshape(-1, 128),
        pair_bias,
        w_out.T,
    )
    dma = pltpu.SemaphoreType.DMA
    both = pl.pallas_call(
        functools.partial(whole_kernel, rows * devices),
        out_shape=jax.ShapeDtypeStruct((rows + w_out.shape[1], out_rows), BF),
        in_specs=[SMEM] + [pl.BlockSpec(memory_space=pl.ANY)] * len(operands),
        out_specs=VMEM,
        scratch_shapes=[pltpu.VMEM(x.shape, x.dtype) for x in operands]
        + [
            pltpu.VMEM((2, HALO, width), BF),
            pltpu.VMEM((rows, width), F32),
            pltpu.VMEM((n_atom, toks, 128), BF),
            pltpu.VMEM((n_atom, toks, 128), BF),
            pltpu.VMEM((n_atom, n_col, toks, 128), BF),
            pltpu.VMEM((n_row, group, n_col, toks, 128), BF),
            pltpu.VMEM((q_rows, 128), BF),
            pltpu.VMEM((group, n_row, out_rows, 128), F32),
            pltpu.VMEM((group, n_row, out_rows, k_cols), F32),
            pltpu.VMEM((2, tile_rows, k_cols), BF),
            pltpu.VMEM((n_col, tile_rows, 128), BF),
            pltpu.VMEM((n_col, tile_rows, 128), BF),
            pltpu.VMEM((group, HD, out_rows), BF),
            pltpu.VMEM((n_atom, HD, out_rows), BF),
            dma((len(operands),)),
            dma((2,)),
            dma((2,)),
            dma((2, n_atom)),
            dma((n_atom,)),
            dma((n_atom,)),
            dma((2, max(n_row, n_col))),
            dma((n_col,)),
            dma((n_row,)),
            dma((n_col,)),
            dma((n_col,)),
            dma((group, n_col)),
            dma((n_atom,)),
        ],
        compiler_params=pltpu.CompilerParams(
            collective_id=0, has_side_effects=True, vmem_limit_bytes=56 << 20
        ),
    )(window_start, *operands)
    return (both[:rows], both[rows:].T)


def solution(mesh):
    placed = (
        P(("atom", "row", "col"), None),
        P(("atom", "row", "col")),
        P(("atom", "row", "col")),
        P(("atom", "row", "col"), None),
        P(("atom", "row", "col"), None),
        P(),
        P("atom", "row", "col"),
        P(),
        P(),
        P(),
        P(),
        P(None, "col"),
    )
    return jax.shard_map(
        shards,
        mesh=mesh,
        in_specs=placed,
        out_specs=(P(("atom", "row", "col"), None), P(("row", "atom"), "col")),
        check_vma=False,
    )
```

```python
import functools

import jax
import jax.numpy as jnp
from jax import lax
from jax.experimental import pallas as pl
from jax.experimental.pallas import tpu as pltpu
from jax.sharding import PartitionSpec as P

AH = 4
QB = 32
KW = 128
HALO = 64
HD = 48
LAST = 80
EPS = 1e-05
NEG = -1e30
BF = jnp.bfloat16
F32 = jnp.float32
MESH = pl.DeviceIdType.MESH
VMEM = pl.BlockSpec(memory_space=pltpu.VMEM)
SMEM = pl.BlockSpec(memory_space=pltpu.SMEM)
NT = (((1,), (1,)), ((), ()))


def layer_norm(values):
    centre = values - jnp.mean(values, axis=-1, keepdims=True)
    spread = jnp.mean(centre * centre, axis=-1, keepdims=True)
    return (centre * lax.rsqrt(spread + EPS)).astype(BF)


def dot(a, b):
    return jnp.dot(a, b, preferred_element_type=F32)


def iota(shape, dim):
    return lax.broadcasted_iota(jnp.int32, shape, dim)


def place():
    return lax.axis_index("atom"), lax.axis_index("row"), lax.axis_index("col")


def project(feats, w_atom_ref, first, last):
    return dot(layer_norm(feats.astype(F32)), w_atom_ref[:, first:last])


def window(b, all_atoms, first_atom, start, query, pairs, bias_ref):
    width = query.shape[1]
    part = width // AH
    lane_head = iota((QB, width), 1) // part
    shift = start - (first_atom + QB * b) + HALO
    reach = pairs.shape[0]
    ahead = iota((KW, reach), 1) - iota((KW, reach), 0)
    pick = jnp.where(ahead == shift, 1.0, 0.0).astype(BF)
    keyed = dot(pick, pairs).astype(BF)
    stacked = jnp.concatenate(
        [jnp.where(lane_head == h, query, jnp.zeros_like(query)) for h in range(AH)], axis=0
    )
    scores = lax.dot_general(stacked, keyed[:, :width], NT, preferred_element_type=F32)
    bias = jnp.concatenate(
        [bias_ref[QB * b : QB * (b + 1), KW * h : KW * (h + 1)] for h in range(AH)], axis=0
    )
    scores = scores * part ** (-0.5) + bias.astype(F32)
    placed = start + iota((1, KW), 1)
    scores = jnp.where((placed >= 0) & (placed < all_atoms), scores, NEG)
    expo = jnp.exp(scores - jnp.max(scores, axis=-1, keepdims=True))
    weights = (expo / jnp.sum(expo, axis=-1, keepdims=True)).astype(BF)
    mixed = dot(weights, keyed[:, width:])
    block = mixed[:QB]
    for h in range(1, AH):
        block = jnp.where(lane_head == h, mixed[QB * h : QB * (h + 1)], block)
    return block


def tokens(member_ref, single_ref, hidden, device):
    toks, rows = single_ref.shape[0], hidden.shape[0]
    local = member_ref[...] - device * toks
    member = jnp.where(local == iota((toks, rows), 0), 1.0, 0.0)
    sums = dot(member.astype(BF), hidden)
    counts = jnp.sum(member, axis=1, keepdims=True)
    return layer_norm(single_ref[...].astype(F32) + sums / counts)


def chooser():
    span = 8 * HD
    source, target = iota((span, 512), 0), iota((span, 512), 1)
    lane = target % 128
    kind = (target // 128) % 2
    base = (target // 256) * 4 * HD
    first = base + jnp.where(kind == 0, 0, HD) + lane
    second = base + jnp.where(kind == 0, 3 * HD, 2 * HD) + lane - LAST
    wanted = jnp.where(lane < HD, first, jnp.where(lane >= LAST, second, -1))
    return jnp.where(source == wanted, 1.0, 0.0).astype(BF)


def tiles(head_data, choose, first, qg_ref, kv_ref):
    toks, columns = head_data.shape
    span = 8 * HD
    pairs = columns // span
    stacked = jnp.concatenate(
        [head_data[:, span * p : span * (p + 1)] for p in range(pairs)], axis=0
    )
    spread = dot(stacked, choose).astype(BF)
    for h in range(2 * pairs):
        rows_h = slice(toks * (h // 2), toks * (h // 2 + 1))
        at = 256 * (h % 2)
        qg_ref[first + h] = spread[rows_h, at : at + 128]
        kv_ref[first + h] = spread[rows_h, at + 128 : at + 256]


def summary(mixed, top):
    lane = iota(mixed.shape, 1)
    total = mixed[:, HD + 1 : HD + 2]
    high = top.astype(BF).astype(F32)
    middle = (top - high).astype(BF).astype(F32)
    total_high = total.astype(BF).astype(F32)
    for at, value in enumerate((high, middle, top - high - middle, total_high, total - total_high)):
        mixed = jnp.where(lane == 64 + at, value, mixed)
    return mixed


def paired(first, second):
    return jnp.where(iota(first.shape, 1) >= 64, first, pltpu.roll(second, 64, 1))


def merged(parts, gates):
    parts = [p.astype(F32) for p in parts]
    scales, totals = [], []
    for at in (64, 0):
        tops = [p[:, at : at + 1] + p[:, at + 1 : at + 2] + p[:, at + 2 : at + 3] for p in parts]
        counts = [p[:, at + 3 : at + 4] + p[:, at + 4 : at + 5] for p in parts]
        top = functools.reduce(jnp.maximum, tops)
        scales.append([jnp.exp(t - top) for t in tops])
        totals.append(sum(s * t for s, t in zip(scales[-1], counts)))
    low = iota(parts[0].shape, 1) >= 64
    mixed = sum(jnp.where(low, s, t) * p for s, t, p in zip(*scales, parts))
    attended = mixed / jnp.where(low, *totals) * jax.nn.sigmoid(gates)
    return jnp.transpose(attended).astype(BF)


def unless(own, remote, local):
    @pl.when(jnp.logical_not(own))
    def _():
        remote()

    @pl.when(own)
    def _():
        local()


def whole_kernel(
    all_atoms,
    start_ref,
    feats_in,
    w_atom_in,
    bias_in,
    w_atom_out_in,
    w_to_token_in,
    member_in,
    single_in,
    w_token_in,
    mask_in,
    pair_in,
    w_out_in,
    out_ref,
    feats_ref,
    w_atom_ref,
    bias_ref,
    w_atom_out_ref,
    w_to_token_ref,
    member_ref,
    single_ref,
    w_token_ref,
    mask_ref,
    pair_ref,
    w_out_ref,
    halo_ref,
    mixed_ref,
    qg_ref,
    kv_ref,
    qown_ref,
    kown_ref,
    qpack_ref,
    gate_ref,
    keys_ref,
    query_ref,
    peak_ref,
    score_ref,
    weight_ref,
    part_ref,
    got_ref,
    head_ref,
    all_ref,
    load,
    halo_send,
    halo_recv,
    send,
    q_sem,
    k_sem,
    g_send,
    gq_sem,
    gk_sem,
    gg_sem,
    m_send,
    m_recv,
    h_send,
    h_recv,
):
    a, r, c = place()
    n_atom, n_row, n_col = (lax.axis_size(x) for x in ("atom", "row", "col"))
    group_q, group_k = n_atom // n_row, n_atom // n_col
    devices = n_atom * n_row * n_col
    device = (a * n_row + r) * n_col + c
    rows = feats_ref.shape[0]
    barrier = pltpu.get_barrier_semaphore()
    loads = [
        pltpu.make_async_copy(source, target, load.at[i])
        for i, (source, target) in enumerate(
            (
                (feats_in, feats_ref),
                (w_atom_in, w_atom_ref),
                (bias_in, bias_ref),
                (w_atom_out_in, w_atom_out_ref),
                (w_to_token_in, w_to_token_ref),
                (member_in, member_ref),
                (single_in, single_ref),
                (w_token_in, w_token_ref),
                (mask_in, mask_ref),
                (pair_in, pair_ref),
                (w_out_in, w_out_ref),
            )
        )
    ]
    for copy in loads[:3]:
        copy.start()

    def signal(to):
        pl.semaphore_signal(barrier, inc=1, device_id=to, device_id_type=MESH)

    own_q = a // group_q == r
    own_k = a // group_k == c
    own_h = lax.rem(a, n_row) == c

    def greet(i, carry):
        signal((i, r, lax.rem(a, n_row)))
        signal((group_k * c + i // n_col, r, lax.rem(i, n_col)))
        signal((group_q * r + i // n_row, lax.rem(i, n_row), c))
        return carry

    lax.fori_loop(0, n_atom, greet, 0)
    for step in range(1, n_col):
        signal((a, r, lax.rem(c + step, n_col)))
    for step in range(1, n_row):
        signal((a, lax.rem(r + step, n_row), c))
    for step in (1, devices - 1):
        other = lax.rem(device + step, devices)
        signal((other // (n_row * n_col), lax.rem(other // n_col, n_row), lax.rem(other, n_col)))

    def halo_copy(side):
        other = lax.rem(device + (1 if side == 0 else devices - 1), devices)
        edge = rows - HALO if side == 0 else 0
        return pltpu.make_async_remote_copy(
            src_ref=feats_in.at[pl.ds(edge, HALO)],
            dst_ref=halo_ref.at[side],
            send_sem=halo_send.at[side],
            recv_sem=halo_recv.at[side],
            device_id=(
                other // (n_row * n_col),
                lax.rem(other // n_col, n_row),
                lax.rem(other, n_col),
            ),
            device_id_type=MESH,
        )

    def drain_halo():
        for side in range(2):
            halo_copy(side).wait_send()

    for copy in loads[:3]:
        copy.wait()
    for copy in loads[3:9]:
        copy.start()
    rows, width = feats_ref.shape
    first_atom = device * rows
    with jax.named_scope("inner_windows"):
        feats = feats_ref[...]
        proj = project(feats, w_atom_ref, 0, 4 * width)
        queries = proj[:, :width].astype(BF)
        pairs = proj[:, width : 3 * width].astype(BF)
        gate = jax.nn.sigmoid(proj[:, 3 * width :])
        edge = HALO // QB
        blocks = rows // QB
        inner = range(edge, blocks - edge)

        def one_window(b, reach):
            query = queries[QB * b : QB * (b + 1)]
            mixed_ref[QB * b : QB * (b + 1)] = window(
                b, all_atoms, first_atom, start_ref[b], query, reach, bias_ref
            )

        for b in inner:
            one_window(b, pairs[QB * (b - edge) : QB * (b + edge + 1)])
    for copy in loads[9:]:
        copy.start()
    with jax.named_scope("barrier"):
        pl.semaphore_wait(barrier, 3 * n_atom + (n_col - 1) + (n_row - 1) + 2)
    with jax.named_scope("halo"):
        for side in range(2):
            halo_copy(side).start()
        for side in range(2):
            halo_copy(side).wait_recv()
    with jax.named_scope("outer_windows"):
        around = project(halo_ref[...].reshape(2 * HALO, width), w_atom_ref, width, 3 * width)
        around = around.astype(BF)
        before, after = around[:HALO], around[HALO:]
        wide = jnp.concatenate([before, pairs[: QB * 2 * edge]], axis=0)
        for b in range(edge):
            one_window(b, wide[QB * b : QB * (b + 2 * edge + 1)])
        wide = jnp.concatenate([pairs[rows - QB * 2 * edge :], after], axis=0)
        for b in range(edge):
            one_window(blocks - edge + b, wide[QB * b : QB * (b + 2 * edge + 1)])
        gated = (mixed_ref[...] * gate).astype(BF)
    with jax.named_scope("tokens"):
        for copy in loads[3:7]:
            copy.wait()
        change = dot(gated, w_atom_out_ref[...])
        out_ref[:rows] = change.astype(BF)
        acted = (feats.astype(F32) + change).astype(BF)
        hidden = jnp.maximum(dot(acted, w_to_token_ref[...]), 0.0).astype(BF)
        normed = tokens(member_ref, single_ref, hidden, device)
        for copy in loads[7:9]:
            copy.wait()
        choose = chooser()

    q_four = lax.rem(a, group_q)
    q_slot = q_four * n_row + r
    k_four = lax.rem(a, group_k)
    k_slot = k_four * n_col + c

    def q_copy(to):
        return pltpu.make_async_remote_copy(
            src_ref=qg_ref.at[to],
            dst_ref=qown_ref.at[q_four, r],
            send_sem=send.at[0, to],
            recv_sem=q_sem.at[q_slot],
            device_id=(to, a // group_q, c),
            device_id_type=MESH,
        )

    def k_copy(to):
        return pltpu.make_async_remote_copy(
            src_ref=kv_ref.at[to],
            dst_ref=kown_ref.at[k_four, c],
            send_sem=send.at[1, to],
            recv_sem=k_sem.at[k_slot],
            device_id=(to, r, a // group_k),
            device_id_type=MESH,
        )

    def drain_tiles():
        def sent(to, carry):
            unless(own_q & (to == a), lambda: q_copy(to).wait_send(), lambda: None)
            unless(own_k & (to == a), lambda: k_copy(to).wait_send(), lambda: None)
            return carry

        lax.fori_loop(0, n_atom, sent, 0)

    half = n_atom // 2
    columns = half * 4 * HD
    for k in range(2):
        first = lax.rem(a // half + 1 + k, 2) * half
        with jax.named_scope("tiles"):
            span = pl.ds(pl.multiple_of(first * 4 * HD, 128), columns)
            head_data = dot(normed, w_token_ref[:, span]).astype(BF)
            tiles(head_data, choose, first, qg_ref, kv_ref)

        def start(i, carry):
            to = first + lax.rem(a + i, half)
            unless(
                own_k & (to == a),
                lambda: k_copy(to).start(),
                lambda: pltpu.make_async_copy(
                    kv_ref.at[to], kown_ref.at[k_four, c], k_sem.at[k_slot]
                ).start(),
            )
            unless(
                own_q & (to == a),
                lambda: q_copy(to).start(),
                lambda: pltpu.make_async_copy(
                    qg_ref.at[to], qown_ref.at[q_four, r], q_sem.at[q_slot]
                ).start(),
            )
            return carry

        with jax.named_scope("send_tiles"):
            lax.fori_loop(0, half, start, 0)

    def arrive_k(i, carry):
        pltpu.make_async_copy(
            kv_ref.at[0], kown_ref.at[i // n_col, lax.rem(i, n_col)], k_sem.at[i]
        ).wait()
        return carry

    def arrive_q(i, carry):
        pltpu.make_async_copy(
            qg_ref.at[0], qown_ref.at[i // n_row, lax.rem(i, n_row)], q_sem.at[i]
        ).wait()
        return carry

    def gather_q(step):
        return pltpu.make_async_remote_copy(
            src_ref=qpack_ref.at[c],
            dst_ref=qpack_ref.at[c],
            send_sem=g_send.at[0, step],
            recv_sem=gq_sem.at[step],
            device_id=(a, r, lax.rem(c + step, n_col)),
            device_id_type=MESH,
        )

    def gather_g(step):
        to = lax.rem(c + step, n_col)
        return pltpu.make_async_remote_copy(
            src_ref=qown_ref.at[:, to],
            dst_ref=gate_ref.at[:, c],
            send_sem=g_send.at[2, step],
            recv_sem=gg_sem.at[step],
            device_id=(a, r, to),
            device_id_type=MESH,
        )

    def partner(step):
        half = n_row // 2
        return lax.rem(r // 2 + step // 2, half) * 2 + lax.rem(lax.rem(r, 2) + step % 2, 2)

    def gather_k(step, value):
        mine = keys_ref.at[r, pl.ds(LAST if value else 0, HD)]
        return pltpu.make_async_remote_copy(
            src_ref=mine,
            dst_ref=mine,
            send_sem=g_send.at[3 + value, step],
            recv_sem=gk_sem.at[value, step],
            device_id=(a, partner(step), c),
            device_id_type=MESH,
        )

    def drain_gather():
        for step in range(1, n_col):
            gather_q(step).wait_send()
            gather_g(step).wait_send()
        for step in range(1, n_row):
            gather_k(step, 0).wait_send()
            gather_k(step, 1).wait_send()

    q_rows, keys = pair_ref.shape[1:]
    per_slot = q_rows // n_atom
    per_row = keys // n_row
    live = jnp.sum(jnp.sum(mask_ref[...], axis=0, keepdims=True), axis=1, keepdims=True)
    kind, column = iota((32, per_row), 0), iota((32, per_row), 1)
    token = (group_k * c + column // per_slot) * per_row + lax.rem(column, per_slot)
    for i in range(n_row):
        masked = jnp.where(token + i * per_slot < live, 0.0, NEG)
        extra = jnp.where(kind == 0, masked, jnp.where(kind == 1, 1.0, 0.0))
        keys_ref[i, HD:LAST] = extra.astype(BF)
    with jax.named_scope("tiles_arrive"):
        lax.fori_loop(0, n_atom, arrive_k, 0)
        moved = jnp.transpose(kown_ref[...].reshape(per_row, 128).astype(F32))
        keys_ref[r, :HD] = moved[:HD].astype(BF)
        keys_ref[r, LAST:] = moved[LAST:].astype(BF)
        for value in range(2):
            for step in range(1, n_row):
                gather_k(step, value).start()
        lax.fori_loop(0, n_atom, arrive_q, 0)
        half = q_rows // n_col // 2
        lane = iota((half, 128), 1)
        low = qown_ref[: group_q // 2].reshape(half, 128).astype(F32)
        high = qown_ref[group_q // 2 :].reshape(half, 128).astype(F32)
        qpack_ref[c] = jnp.where(lane < 64, low, pltpu.roll(high, 64, 1)).astype(BF)
        for step in (2, 1, 3):
            gather_q(step).start()
        for step in range(1, n_col):
            gather_g(step).start()
        gate_ref[:, c] = qown_ref[:, c]
    with jax.named_scope("gather_q"):
        wanted = lane < HD
        one = jnp.where(lane == HD, 1.0, 0.0)
        for step in range(n_col):
            source = lax.rem(c + n_col - step, n_col)
            if step > 0:
                gather_q(step).wait_recv()
            packed = qpack_ref[source].astype(F32)
            for i, value in enumerate((packed, pltpu.roll(packed, 64, 1))):
                value = jnp.where(wanted, value, one).astype(BF)
                slots = slice(n_atom // 2 * i, n_atom // 2 * (i + 1))
                query_ref[slots, source] = value.reshape(n_atom // 2, half * 2 // n_atom, 128)
    for copy in loads[9:]:
        copy.wait()
    peak_ref[...] = jnp.full_like(peak_ref, -jnp.inf)

    def score(step, carry):
        source = partner(step)

        @pl.when(step > 0)
        def _():
            mine = keys_ref.at[source, pl.ds(0, HD)]
            pltpu.make_async_copy(mine, mine, gk_sem.at[0, step]).wait()

        half = q_rows // 2
        span = half // (n_row * per_slot)
        for i in range(2):
            rows = slice(half * i, half * (i + 1))
            fours = slice(span * i, span * (i + 1))
            peak = peak_ref[fours]
            for at in range(0, per_row, 256):
                part = dot(
                    query_ref[n_atom // 2 * i : n_atom // 2 * (i + 1)].reshape(half, 128)[:, :LAST],
                    keys_ref[source, :LAST, at : at + 256],
                )
                for k in range(0, 256, 128):
                    four = (at + k) // 128
                    column = four * per_row + source * 128
                    bias = pair_ref[0, rows, pl.ds(pl.multiple_of(column, 128), 128)]
                    value = part[:, k : k + 128] * HD ** (-0.5) + bias.astype(F32)
                    value = value.reshape(peak.shape)
                    column = source * per_row + at + k
                    score_ref[fours, :, :, pl.ds(pl.multiple_of(column, 128), 128)] = value
                    peak = jnp.maximum(peak, value)
            peak_ref[fours] = peak
        return carry

    with jax.named_scope("scores"):
        lax.fori_loop(0, n_row, score, 0)

    def partial(step):
        to = lax.rem(c + step, n_col)
        return pltpu.make_async_remote_copy(
            src_ref=part_ref.at[to],
            dst_ref=got_ref.at[step],
            send_sem=m_send.at[step],
            recv_sem=m_recv.at[step],
            device_id=(a, r, to),
            device_id_type=MESH,
        )

    def drain_partials():
        for step in range(1, n_col):
            partial(step).wait_send()

    def quarter(i, carry):
        late = i // 2
        step = (1 - late) * (2 - i) + late * (i + 1)
        to = lax.rem(c + step, n_col)
        results = []
        for h in range(2):
            fours = slice(2 * h, 2 * h + 2)
            top = jnp.max(peak_ref[fours, to].reshape(2 * per_slot, 128), axis=1, keepdims=True)
            for at in range(0, keys, 256):
                part = score_ref[fours, to, :, at : at + 256].reshape(2 * per_slot, 256)
                weight_ref[h, :, at : at + 256] = jnp.exp(part - top).astype(BF)
            mixed = sum(
                lax.dot_general(
                    weight_ref[h, :, per_row * k : per_row * (k + 1)],
                    keys_ref[k],
                    NT,
                    preferred_element_type=F32,
                )
                for k in range(n_row)
            )
            results.append(summary(mixed, top))
        part_ref[to] = paired(*results).astype(BF)

        @pl.when(i < n_col - 1)
        def _():
            partial(step).start()

        return carry

    with jax.named_scope("values_arrive"):
        for step in range(1, n_row):
            gather_k(step, 1).wait_recv()
    with jax.named_scope("attention"):
        lax.fori_loop(0, n_col, quarter, 0)
    with jax.named_scope("partials_arrive"):
        for step in range(1, n_col):
            partial(step).wait_recv()
            gather_g(step).wait_recv()

    def head_copy(j, k):
        return pltpu.make_async_remote_copy(
            src_ref=head_ref.at[j],
            dst_ref=all_ref.at[a],
            send_sem=h_send.at[j, k],
            recv_sem=h_recv.at[a],
            device_id=(n_row * j + c, r, lax.rem(c + k, n_col)),
            device_id_type=MESH,
        )

    def drain_heads():
        def sent(j, carry):
            for k in range(1, n_col):
                head_copy(j, k).wait_send()
            unless(
                own_h & (n_row * j + c == a),
                lambda: head_copy(j, 0).wait_send(),
                lambda: None,
            )
            return carry

        lax.fori_loop(0, group_k, sent, 0)

    out_rows = head_ref.shape[2]

    def one_head(j, carry):
        for k in range(1, n_col):
            head_copy(j, k).start()
        unless(
            own_h & (n_row * j + c == a),
            lambda: head_copy(j, 0).start(),
            lambda: pltpu.make_async_copy(head_ref.at[j], all_ref.at[a], h_recv.at[a]).start(),
        )
        return carry

    with jax.named_scope("merge"):
        parts = [part_ref[c]] + [got_ref[step] for step in range(1, n_col)]
        gates = [
            jnp.concatenate(
                [gate_ref[u].reshape(per_slot, 128) for u in (2 * h, 2 * h + 1)], axis=0
            ).astype(F32)
            for h in range(2)
        ]
        attended = merged(parts, paired(*gates))
        for u in range(group_k):
            at = LAST - 64 * (u // 2)
            head_ref[u] = attended[at : at + HD, out_rows * (u % 2) : out_rows * (u % 2 + 1)]
    with jax.named_scope("send_heads"):
        lax.fori_loop(0, group_k, one_head, 0)

    def arrive(i, carry):
        pltpu.make_async_copy(head_ref.at[0], all_ref.at[i], h_recv.at[i]).wait()
        return carry

    with jax.named_scope("heads_arrive"):
        lax.fori_loop(0, n_atom, arrive, 0)
    with jax.named_scope("output"):
        heads = all_ref[...].reshape(n_atom * HD, head_ref.shape[2])
        out_ref[rows:] = dot(w_out_ref[...], heads).astype(BF)

    drain_halo()
    drain_tiles()
    drain_gather()
    drain_partials()
    drain_heads()


def split_kernel(both_ref, update_ref, out_ref):
    rows = update_ref.shape[0]
    update_ref[...] = both_ref[:rows]
    out_ref[...] = both_ref[rows:]


def shards(
    atom_feats,
    atom_to_token,
    window_start,
    atom_bias,
    token_single,
    token_mask,
    pair_bias,
    w_atom,
    w_atom_out,
    w_to_token,
    w_token,
    w_out,
):
    rows, width = atom_feats.shape
    toks = token_single.shape[0]
    axes = ("atom", "row", "col")
    n_atom, n_row, n_col = (lax.axis_size(x) for x in axes)
    devices = n_atom * n_row * n_col
    q_rows, k_cols = pair_bias.shape[1:]
    out_rows = q_rows // n_atom
    group = n_atom // n_col
    tile_rows = q_rows // n_col // 2
    operands = (
        atom_feats,
        w_atom,
        atom_bias,
        w_atom_out,
        w_to_token,
        atom_to_token.reshape(1, rows),
        token_single,
        w_token,
        token_mask.reshape(-1, 128),
        pair_bias,
        w_out.T,
    )
    dma = pltpu.SemaphoreType.DMA
    both = pl.pallas_call(
        functools.partial(whole_kernel, rows * devices),
        out_shape=jax.ShapeDtypeStruct((rows + w_out.shape[1], out_rows), BF),
        in_specs=[SMEM] + [pl.BlockSpec(memory_space=pl.ANY)] * len(operands),
        out_specs=VMEM,
        scratch_shapes=[pltpu.VMEM(x.shape, x.dtype) for x in operands]
        + [
            pltpu.VMEM((2, HALO, width), BF),
            pltpu.VMEM((rows, width), F32),
            pltpu.VMEM((n_atom, toks, 128), BF),
            pltpu.VMEM((n_atom, toks, 128), BF),
            pltpu.VMEM((n_atom // n_row, n_row, toks, 128), BF),
            pltpu.VMEM((group, n_col, toks, 128), BF),
            pltpu.VMEM((n_col, tile_rows, 128), BF),
            pltpu.VMEM((group, n_col, toks, 128), BF),
            pltpu.VMEM((n_row, 128, k_cols // n_row), BF),
            pltpu.VMEM((n_atom, n_col, toks, 128), BF),
            pltpu.VMEM((group, n_row, out_rows, 128), F32),
            pltpu.VMEM((group, n_row, out_rows, k_cols), F32),
            pltpu.VMEM((2, tile_rows, k_cols), BF),
            pltpu.VMEM((n_col, tile_rows, 128), BF),
            pltpu.VMEM((n_col, tile_rows, 128), BF),
            pltpu.VMEM((group, HD, out_rows), BF),
            pltpu.VMEM((n_atom, HD, out_rows), BF),
            dma((len(operands),)),
            dma((2,)),
            dma((2,)),
            dma((2, n_atom)),
            dma((n_atom,)),
            dma((n_atom,)),
            dma((5, max(n_row, n_col))),
            dma((n_col,)),
            dma((2, n_row)),
            dma((n_col,)),
            dma((n_col,)),
            dma((n_col,)),
            dma((group, n_col)),
            dma((n_atom,)),
        ],
        compiler_params=pltpu.CompilerParams(
            collective_id=0, has_side_effects=True, vmem_limit_bytes=56 << 20
        ),
    )(window_start, *operands)
    update, flipped = pl.pallas_call(
        split_kernel,
        out_shape=(
            jax.ShapeDtypeStruct((rows, width), BF),
            jax.ShapeDtypeStruct((w_out.shape[1], out_rows), BF),
        ),
        in_specs=[VMEM],
        out_specs=(VMEM, VMEM),
    )(both)
    return (update, flipped.T)


def solution(mesh):
    placed = (
        P(("atom", "row", "col"), None),
        P(("atom", "row", "col")),
        P(("atom", "row", "col")),
        P(("atom", "row", "col"), None),
        P(("atom", "row", "col"), None),
        P(),
        P("atom", "row", "col"),
        P(),
        P(),
        P(),
        P(),
        P(None, "col"),
    )
    return jax.shard_map(
        shards,
        mesh=mesh,
        in_specs=placed,
        out_specs=(P(("atom", "row", "col"), None), P(("row", "atom"), "col")),
        check_vma=False,
    )
```

```python
import functools

import jax
import jax.numpy as jnp
from jax import lax
from jax.experimental import pallas as pl
from jax.experimental.pallas import tpu as pltpu
from jax.sharding import PartitionSpec as P

AH = 4
QB = 32
KW = 128
HALO = 64
HD = 48
LAST = 80
EPS = 1e-05
NEG = -1e30
BF = jnp.bfloat16
F32 = jnp.float32
MESH = pl.DeviceIdType.MESH
VMEM = pl.BlockSpec(memory_space=pltpu.VMEM)
SMEM = pl.BlockSpec(memory_space=pltpu.SMEM)
NT = (((1,), (1,)), ((), ()))


def layer_norm(values):
    centre = values - jnp.mean(values, axis=-1, keepdims=True)
    spread = jnp.mean(centre * centre, axis=-1, keepdims=True)
    return (centre * lax.rsqrt(spread + EPS)).astype(BF)


def dot(a, b):
    return jnp.dot(a, b, preferred_element_type=F32)


def iota(shape, dim):
    return lax.broadcasted_iota(jnp.int32, shape, dim)


def place():
    return lax.axis_index("atom"), lax.axis_index("row"), lax.axis_index("col")


def window(b, all_atoms, first_atom, start, query, pairs, bias_ref):
    width = query.shape[1]
    part = width // AH
    lane_head = iota((QB, width), 1) // part
    shift = start - (first_atom + QB * b) + HALO
    reach = pairs.shape[0]
    ahead = iota((KW, reach), 1) - iota((KW, reach), 0)
    pick = jnp.where(ahead == shift, 1.0, 0.0).astype(BF)
    keyed = dot(pick, pairs).astype(BF)
    stacked = jnp.concatenate(
        [jnp.where(lane_head == h, query, jnp.zeros_like(query)) for h in range(AH)], axis=0
    )
    scores = lax.dot_general(stacked, keyed[:, :width], NT, preferred_element_type=F32)
    bias = jnp.concatenate(
        [bias_ref[QB * b : QB * (b + 1), KW * h : KW * (h + 1)] for h in range(AH)], axis=0
    )
    scores = scores * part ** (-0.5) + bias.astype(F32)
    placed = start + iota((1, KW), 1)
    scores = jnp.where((placed >= 0) & (placed < all_atoms), scores, NEG)
    expo = jnp.exp(scores - jnp.max(scores, axis=-1, keepdims=True))
    weights = (expo / jnp.sum(expo, axis=-1, keepdims=True)).astype(BF)
    mixed = dot(weights, keyed[:, width:])
    block = mixed[:QB]
    for h in range(1, AH):
        block = jnp.where(lane_head == h, mixed[QB * h : QB * (h + 1)], block)
    return block


def tokens(member_ref, single_ref, hidden, device):
    toks, rows = single_ref.shape[0], hidden.shape[0]
    local = member_ref[...] - device * toks
    member = jnp.where(local == iota((toks, rows), 0), 1.0, 0.0)
    sums = dot(member.astype(BF), hidden)
    counts = jnp.sum(member, axis=1, keepdims=True)
    return layer_norm(single_ref[...].astype(F32) + sums / counts)


def chooser():
    span = 8 * HD
    source, target = iota((span, 512), 0), iota((span, 512), 1)
    lane = target % 128
    kind = (target // 128) % 2
    base = (target // 256) * 4 * HD
    first = base + jnp.where(kind == 0, 0, HD) + lane
    second = base + jnp.where(kind == 0, 3 * HD, 2 * HD) + lane - LAST
    wanted = jnp.where(lane < HD, first, jnp.where(lane >= LAST, second, -1))
    return jnp.where(source == wanted, 1.0, 0.0).astype(BF)


def tiles(head_data, choose, first, qg_ref, kv_ref):
    toks, columns = head_data.shape
    span = 8 * HD
    pairs = columns // span
    stacked = jnp.concatenate(
        [head_data[:, span * p : span * (p + 1)] for p in range(pairs)], axis=0
    )
    spread = dot(stacked, choose).astype(BF)
    for h in range(2 * pairs):
        rows_h = slice(toks * (h // 2), toks * (h // 2 + 1))
        at = 256 * (h % 2)
        qg_ref[first + h] = spread[rows_h, at : at + 128]
        kv_ref[first + h] = spread[rows_h, at + 128 : at + 256]


def summary(mixed, top):
    lane = iota(mixed.shape, 1)
    total = mixed[:, HD + 1 : HD + 2]
    high = top.astype(BF).astype(F32)
    middle = (top - high).astype(BF).astype(F32)
    total_high = total.astype(BF).astype(F32)
    for at, value in enumerate((high, middle, top - high - middle, total_high, total - total_high)):
        mixed = jnp.where(lane == 64 + at, value, mixed)
    return mixed


def paired(first, second):
    return jnp.where(iota(first.shape, 1) >= 64, first, pltpu.roll(second, 64, 1))


def merged(parts, gates):
    parts = [p.astype(F32) for p in parts]
    scales, totals = [], []
    for at in (64, 0):
        tops = [p[:, at : at + 1] + p[:, at + 1 : at + 2] + p[:, at + 2 : at + 3] for p in parts]
        counts = [p[:, at + 3 : at + 4] + p[:, at + 4 : at + 5] for p in parts]
        top = functools.reduce(jnp.maximum, tops)
        scales.append([jnp.exp(t - top) for t in tops])
        totals.append(sum(s * t for s, t in zip(scales[-1], counts)))
    low = iota(parts[0].shape, 1) >= 64
    mixed = sum(jnp.where(low, s, t) * p for s, t, p in zip(*scales, parts))
    attended = mixed / jnp.where(low, *totals) * jax.nn.sigmoid(gates)
    return jnp.transpose(attended).astype(BF)


def unless(own, remote, local):
    @pl.when(jnp.logical_not(own))
    def _():
        remote()

    @pl.when(own)
    def _():
        local()


def whole_kernel(
    all_atoms,
    start_ref,
    feats_in,
    w_atom_in,
    bias_in,
    w_atom_out_in,
    w_to_token_in,
    member_in,
    single_in,
    w_token_in,
    mask_in,
    pair_in,
    w_out_in,
    out_ref,
    feats_ref,
    w_atom_ref,
    bias_ref,
    w_atom_out_ref,
    w_to_token_ref,
    member_ref,
    single_ref,
    w_token_ref,
    mask_ref,
    pair_ref,
    w_out_ref,
    edge_ref,
    halo_ref,
    mixed_ref,
    qg_ref,
    kv_ref,
    qown_ref,
    kown_ref,
    qpack_ref,
    gate_ref,
    keys_ref,
    query_ref,
    peak_ref,
    score_ref,
    weight_ref,
    part_ref,
    got_ref,
    head_ref,
    all_ref,
    load,
    halo_send,
    halo_recv,
    send,
    q_sem,
    k_sem,
    g_send,
    gq_sem,
    gk_sem,
    gg_sem,
    m_send,
    m_recv,
    h_send,
    h_recv,
):
    a, r, c = place()
    n_atom, n_row, n_col = (lax.axis_size(x) for x in ("atom", "row", "col"))
    group_q, group_k = n_atom // n_row, n_atom // n_col
    devices = n_atom * n_row * n_col
    device = (a * n_row + r) * n_col + c
    rows = feats_ref.shape[0]
    barrier = pltpu.get_barrier_semaphore()
    loads = [
        pltpu.make_async_copy(source, target, load.at[i])
        for i, (source, target) in enumerate(
            (
                (feats_in, feats_ref),
                (w_atom_in, w_atom_ref),
                (bias_in, bias_ref),
                (w_atom_out_in, w_atom_out_ref),
                (w_to_token_in, w_to_token_ref),
                (member_in, member_ref),
                (single_in, single_ref),
                (w_token_in, w_token_ref),
                (mask_in, mask_ref),
                (pair_in, pair_ref),
                (w_out_in, w_out_ref),
            )
        )
    ]
    for copy in loads[:3]:
        copy.start()

    def signal(to):
        pl.semaphore_signal(barrier, inc=1, device_id=to, device_id_type=MESH)

    own_q = a // group_q == r
    own_k = a // group_k == c
    own_h = lax.rem(a, n_row) == c

    def greet(i, carry):
        signal((lax.rem(i + n_atom // 2 * (1 - a // (n_atom // 2)), n_atom), r, lax.rem(a, n_row)))
        signal((group_k * c + i // n_col, r, lax.rem(i, n_col)))
        signal((group_q * r + i // n_row, lax.rem(i, n_row), c))
        return carry

    lax.fori_loop(0, n_atom, greet, 0)
    for step in range(1, n_col):
        signal((a, r, lax.rem(c + step, n_col)))
    for step in range(1, n_row):
        signal((a, lax.rem(r + step, n_row), c))
    for step in (1, devices - 1):
        other = lax.rem(device + step, devices)
        signal((other // (n_row * n_col), lax.rem(other // n_col, n_row), lax.rem(other, n_col)))

    def halo_copy(side):
        other = lax.rem(device + (1 if side == 0 else devices - 1), devices)
        return pltpu.make_async_remote_copy(
            src_ref=edge_ref.at[side],
            dst_ref=halo_ref.at[side],
            send_sem=halo_send.at[side],
            recv_sem=halo_recv.at[side],
            device_id=(
                other // (n_row * n_col),
                lax.rem(other // n_col, n_row),
                lax.rem(other, n_col),
            ),
            device_id_type=MESH,
        )

    def drain_halo():
        for side in range(2):
            halo_copy(side).wait_send()

    for copy in loads[:3]:
        copy.wait()
    for copy in loads[3:9]:
        copy.start()
    rows, width = feats_ref.shape
    first_atom = device * rows
    with jax.named_scope("inner_windows"):
        feats = feats_ref[...]
        proj = dot(layer_norm(feats.astype(F32)), w_atom_ref[...])
        queries = proj[:, :width].astype(BF)
        pairs = proj[:, width : 3 * width].astype(BF)
        edge_ref[0] = pairs[rows - HALO :]
        edge_ref[1] = pairs[:HALO]
        gate = jax.nn.sigmoid(proj[:, 3 * width :])
        edge = HALO // QB
        blocks = rows // QB
        inner = range(edge, blocks - edge)

        def one_window(b, reach):
            query = queries[QB * b : QB * (b + 1)]
            mixed_ref[QB * b : QB * (b + 1)] = window(
                b, all_atoms, first_atom, start_ref[b], query, reach, bias_ref
            )

        for b in inner:
            one_window(b, pairs[QB * (b - edge) : QB * (b + edge + 1)])
    for copy in loads[9:]:
        copy.start()
    with jax.named_scope("barrier"):
        pl.semaphore_wait(barrier, 3 * n_atom + (n_col - 1) + (n_row - 1) + 2)
    with jax.named_scope("halo"):
        for side in range(2):
            halo_copy(side).start()
        for side in range(2):
            halo_copy(side).wait_recv()
    with jax.named_scope("outer_windows"):
        before, after = halo_ref[0], halo_ref[1]
        wide = jnp.concatenate([before, pairs[: QB * 2 * edge]], axis=0)
        for b in range(edge):
            one_window(b, wide[QB * b : QB * (b + 2 * edge + 1)])
        wide = jnp.concatenate([pairs[rows - QB * 2 * edge :], after], axis=0)
        for b in range(edge):
            one_window(blocks - edge + b, wide[QB * b : QB * (b + 2 * edge + 1)])
        gated = (mixed_ref[...] * gate).astype(BF)
    with jax.named_scope("tokens"):
        for copy in loads[3:7]:
            copy.wait()
        change = dot(gated, w_atom_out_ref[...])
        out_ref[:rows] = change.astype(BF)
        acted = (feats.astype(F32) + change).astype(BF)
        hidden = jnp.maximum(dot(acted, w_to_token_ref[...]), 0.0).astype(BF)
        normed = tokens(member_ref, single_ref, hidden, device)
        for copy in loads[7:9]:
            copy.wait()
        choose = chooser()

    q_four = lax.rem(a, group_q)
    q_slot = q_four * n_row + r
    k_four = lax.rem(a, group_k)
    k_slot = k_four * n_col + c

    def q_copy(to):
        return pltpu.make_async_remote_copy(
            src_ref=qg_ref.at[to],
            dst_ref=qown_ref.at[q_four, r],
            send_sem=send.at[0, to],
            recv_sem=q_sem.at[q_slot],
            device_id=(to, a // group_q, c),
            device_id_type=MESH,
        )

    def k_copy(to):
        return pltpu.make_async_remote_copy(
            src_ref=kv_ref.at[to],
            dst_ref=kown_ref.at[k_four, c],
            send_sem=send.at[1, to],
            recv_sem=k_sem.at[k_slot],
            device_id=(to, r, a // group_k),
            device_id_type=MESH,
        )

    def drain_tiles():
        def sent(to, carry):
            unless(own_q & (to == a), lambda: q_copy(to).wait_send(), lambda: None)
            unless(own_k & (to == a), lambda: k_copy(to).wait_send(), lambda: None)
            return carry

        lax.fori_loop(0, n_atom, sent, 0)

    half = n_atom // 2
    columns = half * 4 * HD
    for k in range(2):
        first = lax.rem(a // half + 1 + k, 2) * half
        with jax.named_scope("tiles"):
            span = pl.ds(pl.multiple_of(first * 4 * HD, 128), columns)
            head_data = dot(normed, w_token_ref[:, span]).astype(BF)
            tiles(head_data, choose, first, qg_ref, kv_ref)

        def start(i, carry):
            to = first + lax.rem(a + i, half)
            unless(
                own_q & (to == a),
                lambda: q_copy(to).start(),
                lambda: pltpu.make_async_copy(
                    qg_ref.at[to], qown_ref.at[q_four, r], q_sem.at[q_slot]
                ).start(),
            )
            unless(
                own_k & (to == a),
                lambda: k_copy(to).start(),
                lambda: pltpu.make_async_copy(
                    kv_ref.at[to], kown_ref.at[k_four, c], k_sem.at[k_slot]
                ).start(),
            )
            return carry

        with jax.named_scope("send_tiles"):
            lax.fori_loop(0, half, start, 0)

    def arrive_k(i, carry):
        pltpu.make_async_copy(
            kv_ref.at[0], kown_ref.at[i // n_col, lax.rem(i, n_col)], k_sem.at[i]
        ).wait()
        return carry

    def arrive_q(i, carry):
        pltpu.make_async_copy(
            qg_ref.at[0], qown_ref.at[i // n_row, lax.rem(i, n_row)], q_sem.at[i]
        ).wait()
        return carry

    def gather_q(step):
        return pltpu.make_async_remote_copy(
            src_ref=qpack_ref.at[c],
            dst_ref=qpack_ref.at[c],
            send_sem=g_send.at[0, step],
            recv_sem=gq_sem.at[step],
            device_id=(a, r, lax.rem(c + step, n_col)),
            device_id_type=MESH,
        )

    def gather_g(step):
        to = lax.rem(c + step, n_col)
        return pltpu.make_async_remote_copy(
            src_ref=qown_ref.at[:, to],
            dst_ref=gate_ref.at[:, c],
            send_sem=g_send.at[2, step],
            recv_sem=gg_sem.at[step],
            device_id=(a, r, to),
            device_id_type=MESH,
        )

    def partner(step):
        half = n_row // 2
        return lax.rem(r // 2 + step // 2, half) * 2 + lax.rem(lax.rem(r, 2) + step % 2, 2)

    def gather_k(step, value):
        mine = keys_ref.at[r, pl.ds(LAST if value else 0, HD)]
        return pltpu.make_async_remote_copy(
            src_ref=mine,
            dst_ref=mine,
            send_sem=g_send.at[3 + value, step],
            recv_sem=gk_sem.at[value, step],
            device_id=(a, partner(step), c),
            device_id_type=MESH,
        )

    def drain_gather():
        for step in range(1, n_col):
            gather_q(step).wait_send()
            gather_g(step).wait_send()
        for step in range(1, n_row):
            gather_k(step, 0).wait_send()
            gather_k(step, 1).wait_send()

    q_rows, keys = pair_ref.shape[1:]
    per_slot = q_rows // n_atom
    per_row = keys // n_row
    live = jnp.sum(jnp.sum(mask_ref[...], axis=0, keepdims=True), axis=1, keepdims=True)
    kind, column = iota((32, per_row), 0), iota((32, per_row), 1)
    token = (group_k * c + column // per_slot) * per_row + lax.rem(column, per_slot)
    for i in range(n_row):
        masked = jnp.where(token + i * per_slot < live, 0.0, NEG)
        extra = jnp.where(kind == 0, masked, jnp.where(kind == 1, 1.0, 0.0))
        keys_ref[i, HD:LAST] = extra.astype(BF)
    with jax.named_scope("tiles_arrive"):
        lax.fori_loop(0, n_atom, arrive_k, 0)
        moved = jnp.transpose(kown_ref[...].reshape(per_row, 128).astype(F32))
        keys_ref[r, :HD] = moved[:HD].astype(BF)
        keys_ref[r, LAST:] = moved[LAST:].astype(BF)
        for value in range(2):
            for step in range(1, n_row):
                gather_k(step, value).start()
        lax.fori_loop(0, n_atom, arrive_q, 0)
        half = q_rows // n_col // 2
        lane = iota((half, 128), 1)
        low = qown_ref[: group_q // 2].reshape(half, 128).astype(F32)
        high = qown_ref[group_q // 2 :].reshape(half, 128).astype(F32)
        qpack_ref[c] = jnp.where(lane < 64, low, pltpu.roll(high, 64, 1)).astype(BF)
        for step in (2, 1, 3):
            gather_q(step).start()
        for step in range(1, n_col):
            gather_g(step).start()
        gate_ref[:, c] = qown_ref[:, c]
    with jax.named_scope("gather_q"):
        wanted = lane < HD
        one = jnp.where(lane == HD, 1.0, 0.0)
        for step in range(n_col):
            source = lax.rem(c + n_col - step, n_col)
            if step > 0:
                gather_q(step).wait_recv()
            packed = qpack_ref[source].astype(F32)
            for i, value in enumerate((packed, pltpu.roll(packed, 64, 1))):
                value = jnp.where(wanted, value, one).astype(BF)
                slots = slice(n_atom // 2 * i, n_atom // 2 * (i + 1))
                query_ref[slots, source] = value.reshape(n_atom // 2, half * 2 // n_atom, 128)
    for copy in loads[9:]:
        copy.wait()
    peak_ref[...] = jnp.full_like(peak_ref, -jnp.inf)

    def score(step, carry):
        source = partner(step)

        @pl.when(step > 0)
        def _():
            mine = keys_ref.at[source, pl.ds(0, HD)]
            pltpu.make_async_copy(mine, mine, gk_sem.at[0, step]).wait()

        half = q_rows // 2
        span = half // (n_row * per_slot)
        for i in range(2):
            rows = slice(half * i, half * (i + 1))
            fours = slice(span * i, span * (i + 1))
            peak = peak_ref[fours]
            for at in range(0, per_row, 256):
                part = dot(
                    query_ref[n_atom // 2 * i : n_atom // 2 * (i + 1)].reshape(half, 128)[:, :LAST],
                    keys_ref[source, :LAST, at : at + 256],
                )
                for k in range(0, 256, 128):
                    four = (at + k) // 128
                    column = four * per_row + source * 128
                    bias = pair_ref[0, rows, pl.ds(pl.multiple_of(column, 128), 128)]
                    value = part[:, k : k + 128] * HD ** (-0.5) + bias.astype(F32)
                    value = value.reshape(peak.shape)
                    column = source * per_row + at + k
                    score_ref[fours, :, :, pl.ds(pl.multiple_of(column, 128), 128)] = value
                    peak = jnp.maximum(peak, value)
            peak_ref[fours] = peak
        return carry

    with jax.named_scope("scores"):
        lax.fori_loop(0, n_row, score, 0)

    def partial(step):
        to = lax.rem(c + step, n_col)
        return pltpu.make_async_remote_copy(
            src_ref=part_ref.at[to],
            dst_ref=got_ref.at[step],
            send_sem=m_send.at[step],
            recv_sem=m_recv.at[step],
            device_id=(a, r, to),
            device_id_type=MESH,
        )

    def drain_partials():
        for step in range(1, n_col):
            partial(step).wait_send()

    def quarter(i, carry):
        late = i // 2
        step = (1 - late) * (2 - i) + late * (i + 1)
        to = lax.rem(c + step, n_col)
        results = []
        for h in range(2):
            fours = slice(2 * h, 2 * h + 2)
            top = jnp.max(peak_ref[fours, to].reshape(2 * per_slot, 128), axis=1, keepdims=True)
            for at in range(0, keys, 256):
                part = score_ref[fours, to, :, at : at + 256].reshape(2 * per_slot, 256)
                weight_ref[h, :, at : at + 256] = jnp.exp(part - top).astype(BF)
            mixed = sum(
                lax.dot_general(
                    weight_ref[h, :, per_row * k : per_row * (k + 1)],
                    keys_ref[k],
                    NT,
                    preferred_element_type=F32,
                )
                for k in range(n_row)
            )
            results.append(summary(mixed, top))
        part_ref[to] = paired(*results).astype(BF)

        @pl.when(i < n_col - 1)
        def _():
            partial(step).start()

        return carry

    with jax.named_scope("values_arrive"):
        for step in range(1, n_row):
            gather_k(step, 1).wait_recv()
    with jax.named_scope("attention"):
        lax.fori_loop(0, n_col, quarter, 0)
    with jax.named_scope("partials_arrive"):
        for step in range(1, n_col):
            partial(step).wait_recv()
            gather_g(step).wait_recv()

    def head_copy(j, k):
        return pltpu.make_async_remote_copy(
            src_ref=head_ref.at[j],
            dst_ref=all_ref.at[a],
            send_sem=h_send.at[j, k],
            recv_sem=h_recv.at[a],
            device_id=(n_row * j + c, r, lax.rem(c + k, n_col)),
            device_id_type=MESH,
        )

    def drain_heads():
        def sent(j, carry):
            for k in range(1, n_col):
                head_copy(j, k).wait_send()
            unless(
                own_h & (n_row * j + c == a),
                lambda: head_copy(j, 0).wait_send(),
                lambda: None,
            )
            return carry

        lax.fori_loop(0, group_k, sent, 0)

    out_rows = head_ref.shape[2]

    def one_head(i, carry):
        j = lax.rem(i + group_k // 2 * (1 - a // (n_atom // 2)), group_k)
        for k in (2, 1, 3):
            head_copy(j, k).start()
        unless(
            own_h & (n_row * j + c == a),
            lambda: head_copy(j, 0).start(),
            lambda: pltpu.make_async_copy(head_ref.at[j], all_ref.at[a], h_recv.at[a]).start(),
        )
        return carry

    with jax.named_scope("merge"):
        parts = [part_ref[c]] + [got_ref[step] for step in range(1, n_col)]
        gates = [
            jnp.concatenate(
                [gate_ref[u].reshape(per_slot, 128) for u in (2 * h, 2 * h + 1)], axis=0
            ).astype(F32)
            for h in range(2)
        ]
        attended = merged(parts, paired(*gates))
        for u in range(group_k):
            at = LAST - 64 * (u // 2)
            head_ref[u] = attended[at : at + HD, out_rows * (u % 2) : out_rows * (u % 2 + 1)]
    with jax.named_scope("send_heads"):
        lax.fori_loop(0, group_k, one_head, 0)

    def arrive(i, carry):
        pltpu.make_async_copy(head_ref.at[0], all_ref.at[i], h_recv.at[i]).wait()
        return carry

    with jax.named_scope("heads_arrive"):
        lax.fori_loop(0, n_atom, arrive, 0)
    with jax.named_scope("output"):
        heads = all_ref[...].reshape(n_atom * HD, head_ref.shape[2])
        out_ref[rows:] = dot(w_out_ref[...], heads).astype(BF)

    drain_halo()
    drain_tiles()
    drain_gather()
    drain_partials()
    drain_heads()


def split_kernel(both_ref, update_ref, out_ref):
    rows = update_ref.shape[0]
    update_ref[...] = both_ref[:rows]
    out_ref[...] = both_ref[rows:]


def shards(
    atom_feats,
    atom_to_token,
    window_start,
    atom_bias,
    token_single,
    token_mask,
    pair_bias,
    w_atom,
    w_atom_out,
    w_to_token,
    w_token,
    w_out,
):
    rows, width = atom_feats.shape
    toks = token_single.shape[0]
    axes = ("atom", "row", "col")
    n_atom, n_row, n_col = (lax.axis_size(x) for x in axes)
    devices = n_atom * n_row * n_col
    q_rows, k_cols = pair_bias.shape[1:]
    out_rows = q_rows // n_atom
    group = n_atom // n_col
    tile_rows = q_rows // n_col // 2
    operands = (
        atom_feats,
        w_atom,
        atom_bias,
        w_atom_out,
        w_to_token,
        atom_to_token.reshape(1, rows),
        token_single,
        w_token,
        token_mask.reshape(-1, 128),
        pair_bias,
        w_out.T,
    )
    dma = pltpu.SemaphoreType.DMA
    both = pl.pallas_call(
        functools.partial(whole_kernel, rows * devices),
        out_shape=jax.ShapeDtypeStruct((rows + w_out.shape[1], out_rows), BF),
        in_specs=[SMEM] + [pl.BlockSpec(memory_space=pl.ANY)] * len(operands),
        out_specs=VMEM,
        scratch_shapes=[pltpu.VMEM(x.shape, x.dtype) for x in operands]
        + [
            pltpu.VMEM((2, HALO, 2 * width), BF),
            pltpu.VMEM((2, HALO, 2 * width), BF),
            pltpu.VMEM((rows, width), F32),
            pltpu.VMEM((n_atom, toks, 128), BF),
            pltpu.VMEM((n_atom, toks, 128), BF),
            pltpu.VMEM((n_atom // n_row, n_row, toks, 128), BF),
            pltpu.VMEM((group, n_col, toks, 128), BF),
            pltpu.VMEM((n_col, tile_rows, 128), BF),
            pltpu.VMEM((group, n_col, toks, 128), BF),
            pltpu.VMEM((n_row, 128, k_cols // n_row), BF),
            pltpu.VMEM((n_atom, n_col, toks, 128), BF),
            pltpu.VMEM((group, n_row, out_rows, 128), F32),
            pltpu.VMEM((group, n_row, out_rows, k_cols), F32),
            pltpu.VMEM((2, tile_rows, k_cols), BF),
            pltpu.VMEM((n_col, tile_rows, 128), BF),
            pltpu.VMEM((n_col, tile_rows, 128), BF),
            pltpu.VMEM((group, HD, out_rows), BF),
            pltpu.VMEM((n_atom, HD, out_rows), BF),
            dma((len(operands),)),
            dma((2,)),
            dma((2,)),
            dma((2, n_atom)),
            dma((n_atom,)),
            dma((n_atom,)),
            dma((5, max(n_row, n_col))),
            dma((n_col,)),
            dma((2, n_row)),
            dma((n_col,)),
            dma((n_col,)),
            dma((n_col,)),
            dma((group, n_col)),
            dma((n_atom,)),
        ],
        compiler_params=pltpu.CompilerParams(
            collective_id=0, has_side_effects=True, vmem_limit_bytes=56 << 20
        ),
    )(window_start, *operands)
    update, flipped = pl.pallas_call(
        split_kernel,
        out_shape=(
            jax.ShapeDtypeStruct((rows, width), BF),
            jax.ShapeDtypeStruct((w_out.shape[1], out_rows), BF),
        ),
        in_specs=[VMEM],
        out_specs=(VMEM, VMEM),
    )(both)
    return (update, flipped.T)


def solution(mesh):
    placed = (
        P(("atom", "row", "col"), None),
        P(("atom", "row", "col")),
        P(("atom", "row", "col")),
        P(("atom", "row", "col"), None),
        P(("atom", "row", "col"), None),
        P(),
        P("atom", "row", "col"),
        P(),
        P(),
        P(),
        P(),
        P(None, "col"),
    )
    return jax.shard_map(
        shards,
        mesh=mesh,
        in_specs=placed,
        out_specs=(P(("atom", "row", "col"), None), P(("row", "atom"), "col")),
        check_vma=False,
    )
```

```python
import functools

import jax
import jax.numpy as jnp
from jax import lax
from jax.experimental import pallas as pl
from jax.experimental.pallas import tpu as pltpu
from jax.sharding import PartitionSpec as P

AH = 4
QB = 32
KW = 128
HALO = 64
HD = 48
LAST = 80
EPS = 1e-05
NEG = -1e30
BF = jnp.bfloat16
F32 = jnp.float32
MESH = pl.DeviceIdType.MESH
VMEM = pl.BlockSpec(memory_space=pltpu.VMEM)
SMEM = pl.BlockSpec(memory_space=pltpu.SMEM)
NT = (((1,), (1,)), ((), ()))


def layer_norm(values):
    centre = values - jnp.mean(values, axis=-1, keepdims=True)
    spread = jnp.mean(centre * centre, axis=-1, keepdims=True)
    return (centre * lax.rsqrt(spread + EPS)).astype(BF)


def dot(a, b):
    return jnp.dot(a, b, preferred_element_type=F32)


def iota(shape, dim):
    return lax.broadcasted_iota(jnp.int32, shape, dim)


def place():
    return lax.axis_index("atom"), lax.axis_index("row"), lax.axis_index("col")


def project(feats, w_atom_ref, first, last):
    return dot(layer_norm(feats.astype(F32)), w_atom_ref[:, first:last])


def window(b, all_atoms, first_atom, start, query, pairs, bias_ref):
    width = query.shape[1]
    part = width // AH
    lane_head = iota((QB, width), 1) // part
    shift = start - (first_atom + QB * b) + HALO
    reach = pairs.shape[0]
    ahead = iota((KW, reach), 1) - iota((KW, reach), 0)
    pick = jnp.where(ahead == shift, 1.0, 0.0).astype(BF)
    keyed = dot(pick, pairs).astype(BF)
    stacked = jnp.concatenate(
        [jnp.where(lane_head == h, query, jnp.zeros_like(query)) for h in range(AH)], axis=0
    )
    scores = lax.dot_general(stacked, keyed[:, :width], NT, preferred_element_type=F32)
    bias = jnp.concatenate(
        [bias_ref[QB * b : QB * (b + 1), KW * h : KW * (h + 1)] for h in range(AH)], axis=0
    )
    scores = scores * part ** (-0.5) + bias.astype(F32)
    placed = start + iota((1, KW), 1)
    scores = jnp.where((placed >= 0) & (placed < all_atoms), scores, NEG)
    expo = jnp.exp(scores - jnp.max(scores, axis=-1, keepdims=True))
    weights = (expo / jnp.sum(expo, axis=-1, keepdims=True)).astype(BF)
    mixed = dot(weights, keyed[:, width:])
    block = mixed[:QB]
    for h in range(1, AH):
        block = jnp.where(lane_head == h, mixed[QB * h : QB * (h + 1)], block)
    return block


def tokens(member_ref, single_ref, hidden, device):
    toks, rows = single_ref.shape[0], hidden.shape[0]
    local = member_ref[...] - device * toks
    member = jnp.where(local == iota((toks, rows), 0), 1.0, 0.0)
    sums = dot(member.astype(BF), hidden)
    counts = jnp.sum(member, axis=1, keepdims=True)
    return layer_norm(single_ref[...].astype(F32) + sums / counts)


def chooser():
    span = 8 * HD
    source, target = iota((span, 512), 0), iota((span, 512), 1)
    lane = target % 128
    kind = (target // 128) % 2
    base = (target // 256) * 4 * HD
    first = base + jnp.where(kind == 0, 0, HD) + lane
    second = base + jnp.where(kind == 0, 3 * HD, 2 * HD) + lane - LAST
    wanted = jnp.where(lane < HD, first, jnp.where(lane >= LAST, second, -1))
    return jnp.where(source == wanted, 1.0, 0.0).astype(BF)


def tiles(head_data, choose, first, qg_ref, kv_ref):
    toks, columns = head_data.shape
    span = 8 * HD
    pairs = columns // span
    stacked = jnp.concatenate(
        [head_data[:, span * p : span * (p + 1)] for p in range(pairs)], axis=0
    )
    spread = dot(stacked, choose).astype(BF)
    for h in range(2 * pairs):
        rows_h = slice(toks * (h // 2), toks * (h // 2 + 1))
        at = 256 * (h % 2)
        qg_ref[first + h] = spread[rows_h, at : at + 128]
        kv_ref[first + h] = spread[rows_h, at + 128 : at + 256]


def summary(mixed, top):
    lane = iota(mixed.shape, 1)
    total = mixed[:, HD + 1 : HD + 2]
    high = top.astype(BF).astype(F32)
    middle = (top - high).astype(BF).astype(F32)
    total_high = total.astype(BF).astype(F32)
    for at, value in enumerate((high, middle, top - high - middle, total_high, total - total_high)):
        mixed = jnp.where(lane == 64 + at, value, mixed)
    return mixed


def paired(first, second):
    return jnp.where(iota(first.shape, 1) >= 64, first, pltpu.roll(second, 64, 1))


def merged(parts, gates):
    parts = [p.astype(F32) for p in parts]
    scales, totals = [], []
    for at in (64, 0):
        tops = [p[:, at : at + 1] + p[:, at + 1 : at + 2] + p[:, at + 2 : at + 3] for p in parts]
        counts = [p[:, at + 3 : at + 4] + p[:, at + 4 : at + 5] for p in parts]
        top = functools.reduce(jnp.maximum, tops)
        scales.append([jnp.exp(t - top) for t in tops])
        totals.append(sum(s * t for s, t in zip(scales[-1], counts)))
    low = iota(parts[0].shape, 1) >= 64
    mixed = sum(jnp.where(low, s, t) * p for s, t, p in zip(*scales, parts))
    attended = mixed / jnp.where(low, *totals) * jax.nn.sigmoid(gates)
    return jnp.transpose(attended).astype(BF)


def unless(own, remote, local):
    @pl.when(jnp.logical_not(own))
    def _():
        remote()

    @pl.when(own)
    def _():
        local()


def whole_kernel(
    all_atoms,
    start_ref,
    feats_in,
    w_atom_in,
    bias_in,
    w_atom_out_in,
    w_to_token_in,
    member_in,
    single_in,
    w_token_in,
    mask_in,
    pair_in,
    w_out_in,
    out_ref,
    feats_ref,
    w_atom_ref,
    bias_ref,
    w_atom_out_ref,
    w_to_token_ref,
    member_ref,
    single_ref,
    w_token_ref,
    mask_ref,
    pair_ref,
    w_out_ref,
    halo_ref,
    mixed_ref,
    qg_ref,
    kv_ref,
    qown_ref,
    kown_ref,
    qpack_ref,
    gate_ref,
    keys_ref,
    query_ref,
    peak_ref,
    score_ref,
    weight_ref,
    part_ref,
    got_ref,
    head_ref,
    all_ref,
    load,
    halo_send,
    halo_recv,
    send,
    q_sem,
    k_sem,
    g_send,
    gq_sem,
    gk_sem,
    gg_sem,
    m_send,
    m_recv,
    h_send,
    h_recv,
):
    a, r, c = place()
    n_atom, n_row, n_col = (lax.axis_size(x) for x in ("atom", "row", "col"))
    group_q, group_k = n_atom // n_row, n_atom // n_col
    devices = n_atom * n_row * n_col
    device = (a * n_row + r) * n_col + c
    rows = feats_ref.shape[0]
    barrier = pltpu.get_barrier_semaphore()
    loads = [
        pltpu.make_async_copy(source, target, load.at[i])
        for i, (source, target) in enumerate(
            (
                (feats_in, feats_ref),
                (w_atom_in, w_atom_ref),
                (bias_in, bias_ref),
                (w_atom_out_in, w_atom_out_ref),
                (w_to_token_in, w_to_token_ref),
                (member_in, member_ref),
                (single_in, single_ref),
                (w_token_in, w_token_ref),
                (mask_in, mask_ref),
                (pair_in, pair_ref),
                (w_out_in, w_out_ref),
            )
        )
    ]
    for copy in loads[:3]:
        copy.start()

    def signal(to):
        pl.semaphore_signal(barrier, inc=1, device_id=to, device_id_type=MESH)

    own_q = a // group_q == r
    own_k = a // group_k == c
    own_h = lax.rem(a, n_row) == c

    def greet(i, carry):
        signal((i, r, lax.rem(a, n_row)))
        signal((group_k * c + i // n_col, r, lax.rem(i, n_col)))
        signal((group_q * r + i // n_row, lax.rem(i, n_row), c))
        return carry

    lax.fori_loop(0, n_atom, greet, 0)
    for step in range(1, n_col):
        signal((a, r, lax.rem(c + step, n_col)))
    for step in range(1, n_row):
        signal((a, lax.rem(r + step, n_row), c))
    for step in (1, devices - 1):
        other = lax.rem(device + step, devices)
        signal((other // (n_row * n_col), lax.rem(other // n_col, n_row), lax.rem(other, n_col)))

    def halo_copy(side):
        other = lax.rem(device + (1 if side == 0 else devices - 1), devices)
        edge = rows - HALO if side == 0 else 0
        return pltpu.make_async_remote_copy(
            src_ref=feats_in.at[pl.ds(edge, HALO)],
            dst_ref=halo_ref.at[side],
            send_sem=halo_send.at[side],
            recv_sem=halo_recv.at[side],
            device_id=(
                other // (n_row * n_col),
                lax.rem(other // n_col, n_row),
                lax.rem(other, n_col),
            ),
            device_id_type=MESH,
        )

    def drain_halo():
        for side in range(2):
            halo_copy(side).wait_send()

    for copy in loads[:3]:
        copy.wait()
    for copy in loads[3:9]:
        copy.start()
    rows, width = feats_ref.shape
    first_atom = device * rows
    with jax.named_scope("inner_windows"):
        feats = feats_ref[...]
        proj = project(feats, w_atom_ref, 0, 4 * width)
        queries = proj[:, :width].astype(BF)
        pairs = proj[:, width : 3 * width].astype(BF)
        gate = jax.nn.sigmoid(proj[:, 3 * width :])
        edge = HALO // QB
        blocks = rows // QB
        inner = range(edge, blocks - edge)

        def one_window(b, reach):
            query = queries[QB * b : QB * (b + 1)]
            mixed_ref[QB * b : QB * (b + 1)] = window(
                b, all_atoms, first_atom, start_ref[b], query, reach, bias_ref
            )

        for b in inner:
            one_window(b, pairs[QB * (b - edge) : QB * (b + edge + 1)])
    for copy in loads[9:]:
        copy.start()
    with jax.named_scope("barrier"):
        pl.semaphore_wait(barrier, 3 * n_atom + (n_col - 1) + (n_row - 1) + 2)
    with jax.named_scope("halo"):
        for side in range(2):
            halo_copy(side).start()
        for side in range(2):
            halo_copy(side).wait_recv()
    with jax.named_scope("outer_windows"):
        around = project(halo_ref[...].reshape(2 * HALO, width), w_atom_ref, width, 3 * width)
        around = around.astype(BF)
        before, after = around[:HALO], around[HALO:]
        wide = jnp.concatenate([before, pairs[: QB * 2 * edge]], axis=0)
        for b in range(edge):
            one_window(b, wide[QB * b : QB * (b + 2 * edge + 1)])
        wide = jnp.concatenate([pairs[rows - QB * 2 * edge :], after], axis=0)
        for b in range(edge):
            one_window(blocks - edge + b, wide[QB * b : QB * (b + 2 * edge + 1)])
        gated = (mixed_ref[...] * gate).astype(BF)
    with jax.named_scope("tokens"):
        for copy in loads[3:7]:
            copy.wait()
        change = dot(gated, w_atom_out_ref[...])
        out_ref[:rows] = change.astype(BF)
        acted = (feats.astype(F32) + change).astype(BF)
        hidden = jnp.maximum(dot(acted, w_to_token_ref[...]), 0.0).astype(BF)
        normed = tokens(member_ref, single_ref, hidden, device)
        for copy in loads[7:9]:
            copy.wait()
        choose = chooser()

    q_four = lax.rem(a, group_q)
    q_slot = q_four * n_row + r
    k_four = lax.rem(a, group_k)
    k_slot = k_four * n_col + c

    def q_copy(to):
        return pltpu.make_async_remote_copy(
            src_ref=qg_ref.at[to],
            dst_ref=qown_ref.at[q_four, r],
            send_sem=send.at[0, to],
            recv_sem=q_sem.at[q_slot],
            device_id=(to, a // group_q, c),
            device_id_type=MESH,
        )

    def k_copy(to):
        return pltpu.make_async_remote_copy(
            src_ref=kv_ref.at[to],
            dst_ref=kown_ref.at[k_four, c],
            send_sem=send.at[1, to],
            recv_sem=k_sem.at[k_slot],
            device_id=(to, r, a // group_k),
            device_id_type=MESH,
        )

    def drain_tiles():
        def sent(to, carry):
            unless(own_q & (to == a), lambda: q_copy(to).wait_send(), lambda: None)
            unless(own_k & (to == a), lambda: k_copy(to).wait_send(), lambda: None)
            return carry

        lax.fori_loop(0, n_atom, sent, 0)

    half = n_atom // 2
    columns = half * 4 * HD
    for k in range(2):
        first = lax.rem(a // half + 1 + k, 2) * half
        with jax.named_scope("tiles"):
            span = pl.ds(pl.multiple_of(first * 4 * HD, 128), columns)
            head_data = dot(normed, w_token_ref[:, span]).astype(BF)
            tiles(head_data, choose, first, qg_ref, kv_ref)

        def start(i, carry):
            to = first + lax.rem(a + i, half)
            unless(
                own_k & (to == a),
                lambda: k_copy(to).start(),
                lambda: pltpu.make_async_copy(
                    kv_ref.at[to], kown_ref.at[k_four, c], k_sem.at[k_slot]
                ).start(),
            )
            unless(
                own_q & (to == a),
                lambda: q_copy(to).start(),
                lambda: pltpu.make_async_copy(
                    qg_ref.at[to], qown_ref.at[q_four, r], q_sem.at[q_slot]
                ).start(),
            )
            return carry

        with jax.named_scope("send_tiles"):
            lax.fori_loop(0, half, start, 0)

    def arrive_k(i, carry):
        pltpu.make_async_copy(
            kv_ref.at[0], kown_ref.at[i // n_col, lax.rem(i, n_col)], k_sem.at[i]
        ).wait()
        return carry

    def arrive_q(i, carry):
        pltpu.make_async_copy(
            qg_ref.at[0], qown_ref.at[i // n_row, lax.rem(i, n_row)], q_sem.at[i]
        ).wait()
        return carry

    def gather_q(step):
        return pltpu.make_async_remote_copy(
            src_ref=qpack_ref.at[c],
            dst_ref=qpack_ref.at[c],
            send_sem=g_send.at[0, step],
            recv_sem=gq_sem.at[step],
            device_id=(a, r, lax.rem(c + step, n_col)),
            device_id_type=MESH,
        )

    def gather_g(step):
        to = lax.rem(c + step, n_col)
        return pltpu.make_async_remote_copy(
            src_ref=qown_ref.at[:, to],
            dst_ref=gate_ref.at[:, c],
            send_sem=g_send.at[2, step],
            recv_sem=gg_sem.at[step],
            device_id=(a, r, to),
            device_id_type=MESH,
        )

    def partner(step):
        half = n_row // 2
        return lax.rem(r // 2 + step // 2, half) * 2 + lax.rem(lax.rem(r, 2) + step % 2, 2)

    def gather_k(step, value):
        mine = keys_ref.at[r, pl.ds(LAST if value else 0, HD)]
        return pltpu.make_async_remote_copy(
            src_ref=mine,
            dst_ref=mine,
            send_sem=g_send.at[3 + value, step],
            recv_sem=gk_sem.at[value, step],
            device_id=(a, partner(step), c),
            device_id_type=MESH,
        )

    def drain_gather():
        for step in range(1, n_col):
            gather_q(step).wait_send()
            gather_g(step).wait_send()
        for step in range(1, n_row):
            gather_k(step, 0).wait_send()
            gather_k(step, 1).wait_send()

    q_rows, keys = pair_ref.shape[1:]
    per_slot = q_rows // n_atom
    per_row = keys // n_row
    live = jnp.sum(jnp.sum(mask_ref[...], axis=0, keepdims=True), axis=1, keepdims=True)
    kind, column = iota((32, per_row), 0), iota((32, per_row), 1)
    token = (group_k * c + column // per_slot) * per_row + lax.rem(column, per_slot)
    for i in range(n_row):
        masked = jnp.where(token + i * per_slot < live, 0.0, NEG)
        extra = jnp.where(kind == 0, masked, jnp.where(kind == 1, 1.0, 0.0))
        keys_ref[i, HD:LAST] = extra.astype(BF)
    with jax.named_scope("tiles_arrive"):
        lax.fori_loop(0, n_atom, arrive_k, 0)
        moved = jnp.transpose(kown_ref[...].reshape(per_row, 128).astype(F32))
        keys_ref[r, :HD] = moved[:HD].astype(BF)
        keys_ref[r, LAST:] = moved[LAST:].astype(BF)
        for value in range(2):
            for step in range(1, n_row):
                gather_k(step, value).start()
        lax.fori_loop(0, n_atom, arrive_q, 0)
        half = q_rows // n_col // 2
        lane = iota((half, 128), 1)
        low = qown_ref[: group_q // 2].reshape(half, 128).astype(F32)
        high = qown_ref[group_q // 2 :].reshape(half, 128).astype(F32)
        qpack_ref[c] = jnp.where(lane < 64, low, pltpu.roll(high, 64, 1)).astype(BF)
        for step in (2, 1, 3):
            gather_q(step).start()
        for step in range(1, n_col):
            gather_g(step).start()
        gate_ref[:, c] = qown_ref[:, c]
    with jax.named_scope("gather_q"):
        wanted = lane < HD
        one = jnp.where(lane == HD, 1.0, 0.0)
        for step in range(n_col):
            source = lax.rem(c + n_col - step, n_col)
            if step > 0:
                gather_q(step).wait_recv()
            packed = qpack_ref[source].astype(F32)
            for i, value in enumerate((packed, pltpu.roll(packed, 64, 1))):
                value = jnp.where(wanted, value, one).astype(BF)
                slots = slice(n_atom // 2 * i, n_atom // 2 * (i + 1))
                query_ref[slots, source] = value.reshape(n_atom // 2, half * 2 // n_atom, 128)
    for copy in loads[9:]:
        copy.wait()
    peak_ref[...] = jnp.full_like(peak_ref, -jnp.inf)

    def score(step, carry):
        source = partner(step)

        @pl.when(step > 0)
        def _():
            mine = keys_ref.at[source, pl.ds(0, HD)]
            pltpu.make_async_copy(mine, mine, gk_sem.at[0, step]).wait()

        half = q_rows // 2
        span = half // (n_row * per_slot)
        for i in range(2):
            rows = slice(half * i, half * (i + 1))
            fours = slice(span * i, span * (i + 1))
            peak = peak_ref[fours]
            for at in range(0, per_row, 256):
                part = dot(
                    query_ref[n_atom // 2 * i : n_atom // 2 * (i + 1)].reshape(half, 128)[:, :LAST],
                    keys_ref[source, :LAST, at : at + 256],
                )
                for k in range(0, 256, 128):
                    four = (at + k) // 128
                    column = four * per_row + source * 128
                    bias = pair_ref[0, rows, pl.ds(pl.multiple_of(column, 128), 128)]
                    value = part[:, k : k + 128] * HD ** (-0.5) + bias.astype(F32)
                    value = value.reshape(peak.shape)
                    column = source * per_row + at + k
                    score_ref[fours, :, :, pl.ds(pl.multiple_of(column, 128), 128)] = value
                    peak = jnp.maximum(peak, value)
            peak_ref[fours] = peak
        return carry

    with jax.named_scope("scores"):
        lax.fori_loop(0, n_row, score, 0)

    def partial(step):
        to = lax.rem(c + step, n_col)
        return pltpu.make_async_remote_copy(
            src_ref=part_ref.at[to],
            dst_ref=got_ref.at[step],
            send_sem=m_send.at[step],
            recv_sem=m_recv.at[step],
            device_id=(a, r, to),
            device_id_type=MESH,
        )

    def drain_partials():
        for step in range(1, n_col):
            partial(step).wait_send()

    def quarter(i, carry):
        late = i // 2
        step = (1 - late) * (2 - i) + late * (i + 1)
        to = lax.rem(c + step, n_col)
        tops = [
            jnp.max(peak_ref[2 * h : 2 * h + 2, to].reshape(2 * per_slot, 128), axis=1, keepdims=True)
            for h in range(2)
        ]
        mixed = None
        for k in range(n_row):
            for h in range(2):
                for at in range(per_row * k, per_row * (k + 1), 256):
                    part = score_ref[2 * h : 2 * h + 2, to, :, at : at + 256]
                    part = jnp.exp(part.reshape(2 * per_slot, 256) - tops[h])
                    weight_ref[h, :, at : at + 256] = part.astype(BF)
            weights = weight_ref[:, :, per_row * k : per_row * (k + 1)]
            piece = lax.dot_general(
                weights.reshape(4 * per_slot, per_row),
                keys_ref[k],
                NT,
                preferred_element_type=F32,
            )
            mixed = piece if mixed is None else mixed + piece
        results = [
            summary(mixed[2 * per_slot * h : 2 * per_slot * (h + 1)], tops[h]) for h in range(2)
        ]
        part_ref[to] = paired(*results).astype(BF)

        @pl.when(i < n_col - 1)
        def _():
            partial(step).start()

        return carry

    with jax.named_scope("values_arrive"):
        for step in range(1, n_row):
            gather_k(step, 1).wait_recv()
    with jax.named_scope("attention"):
        lax.fori_loop(0, n_col, quarter, 0)
    with jax.named_scope("partials_arrive"):
        for step in range(1, n_col):
            partial(step).wait_recv()
            gather_g(step).wait_recv()

    def head_copy(j, k):
        return pltpu.make_async_remote_copy(
            src_ref=head_ref.at[j],
            dst_ref=all_ref.at[a],
            send_sem=h_send.at[j, k],
            recv_sem=h_recv.at[a],
            device_id=(n_row * j + c, r, lax.rem(c + k, n_col)),
            device_id_type=MESH,
        )

    def drain_heads():
        def sent(j, carry):
            for k in range(1, n_col):
                head_copy(j, k).wait_send()
            unless(
                own_h & (n_row * j + c == a),
                lambda: head_copy(j, 0).wait_send(),
                lambda: None,
            )
            return carry

        lax.fori_loop(0, group_k, sent, 0)

    out_rows = head_ref.shape[2]

    def one_head(j, carry):
        for k in range(1, n_col):
            head_copy(j, k).start()
        unless(
            own_h & (n_row * j + c == a),
            lambda: head_copy(j, 0).start(),
            lambda: pltpu.make_async_copy(head_ref.at[j], all_ref.at[a], h_recv.at[a]).start(),
        )
        return carry

    with jax.named_scope("merge"):
        parts = [part_ref[c]] + [got_ref[step] for step in range(1, n_col)]
        gates = [
            jnp.concatenate(
                [gate_ref[u].reshape(per_slot, 128) for u in (2 * h, 2 * h + 1)], axis=0
            ).astype(F32)
            for h in range(2)
        ]
        attended = merged(parts, paired(*gates))
        for u in range(group_k):
            at = LAST - 64 * (u // 2)
            head_ref[u] = attended[at : at + HD, out_rows * (u % 2) : out_rows * (u % 2 + 1)]
    with jax.named_scope("send_heads"):
        lax.fori_loop(0, group_k, one_head, 0)

    def arrive(i, carry):
        pltpu.make_async_copy(head_ref.at[0], all_ref.at[i], h_recv.at[i]).wait()
        return carry

    with jax.named_scope("heads_arrive"):
        lax.fori_loop(0, n_atom, arrive, 0)
    with jax.named_scope("output"):
        heads = all_ref[...].reshape(n_atom * HD, head_ref.shape[2])
        out_ref[rows:] = dot(w_out_ref[...], heads).astype(BF)

    drain_halo()
    drain_tiles()
    drain_gather()
    drain_partials()
    drain_heads()


def split_kernel(both_ref, update_ref, out_ref):
    rows = update_ref.shape[0]
    update_ref[...] = both_ref[:rows]
    out_ref[...] = both_ref[rows:]


def shards(
    atom_feats,
    atom_to_token,
    window_start,
    atom_bias,
    token_single,
    token_mask,
    pair_bias,
    w_atom,
    w_atom_out,
    w_to_token,
    w_token,
    w_out,
):
    rows, width = atom_feats.shape
    toks = token_single.shape[0]
    axes = ("atom", "row", "col")
    n_atom, n_row, n_col = (lax.axis_size(x) for x in axes)
    devices = n_atom * n_row * n_col
    q_rows, k_cols = pair_bias.shape[1:]
    out_rows = q_rows // n_atom
    group = n_atom // n_col
    tile_rows = q_rows // n_col // 2
    operands = (
        atom_feats,
        w_atom,
        atom_bias,
        w_atom_out,
        w_to_token,
        atom_to_token.reshape(1, rows),
        token_single,
        w_token,
        token_mask.reshape(-1, 128),
        pair_bias,
        w_out.T,
    )
    dma = pltpu.SemaphoreType.DMA
    both = pl.pallas_call(
        functools.partial(whole_kernel, rows * devices),
        out_shape=jax.ShapeDtypeStruct((rows + w_out.shape[1], out_rows), BF),
        in_specs=[SMEM] + [pl.BlockSpec(memory_space=pl.ANY)] * len(operands),
        out_specs=VMEM,
        scratch_shapes=[pltpu.VMEM(x.shape, x.dtype) for x in operands]
        + [
            pltpu.VMEM((2, HALO, width), BF),
            pltpu.VMEM((rows, width), F32),
            pltpu.VMEM((n_atom, toks, 128), BF),
            pltpu.VMEM((n_atom, toks, 128), BF),
            pltpu.VMEM((n_atom // n_row, n_row, toks, 128), BF),
            pltpu.VMEM((group, n_col, toks, 128), BF),
            pltpu.VMEM((n_col, tile_rows, 128), BF),
            pltpu.VMEM((group, n_col, toks, 128), BF),
            pltpu.VMEM((n_row, 128, k_cols // n_row), BF),
            pltpu.VMEM((n_atom, n_col, toks, 128), BF),
            pltpu.VMEM((group, n_row, out_rows, 128), F32),
            pltpu.VMEM((group, n_row, out_rows, k_cols), F32),
            pltpu.VMEM((2, tile_rows, k_cols), BF),
            pltpu.VMEM((n_col, tile_rows, 128), BF),
            pltpu.VMEM((n_col, tile_rows, 128), BF),
            pltpu.VMEM((group, HD, out_rows), BF),
            pltpu.VMEM((n_atom, HD, out_rows), BF),
            dma((len(operands),)),
            dma((2,)),
            dma((2,)),
            dma((2, n_atom)),
            dma((n_atom,)),
            dma((n_atom,)),
            dma((5, max(n_row, n_col))),
            dma((n_col,)),
            dma((2, n_row)),
            dma((n_col,)),
            dma((n_col,)),
            dma((n_col,)),
            dma((group, n_col)),
            dma((n_atom,)),
        ],
        compiler_params=pltpu.CompilerParams(
            collective_id=0, has_side_effects=True, vmem_limit_bytes=56 << 20
        ),
    )(window_start, *operands)
    update, flipped = pl.pallas_call(
        split_kernel,
        out_shape=(
            jax.ShapeDtypeStruct((rows, width), BF),
            jax.ShapeDtypeStruct((w_out.shape[1], out_rows), BF),
        ),
        in_specs=[VMEM],
        out_specs=(VMEM, VMEM),
    )(both)
    return (update, flipped.T)


def solution(mesh):
    placed = (
        P(("atom", "row", "col"), None),
        P(("atom", "row", "col")),
        P(("atom", "row", "col")),
        P(("atom", "row", "col"), None),
        P(("atom", "row", "col"), None),
        P(),
        P("atom", "row", "col"),
        P(),
        P(),
        P(),
        P(),
        P(None, "col"),
    )
    return jax.shard_map(
        shards,
        mesh=mesh,
        in_specs=placed,
        out_specs=(P(("atom", "row", "col"), None), P(("row", "atom"), "col")),
        check_vma=False,
    )
```

```python
import functools

import jax
import jax.numpy as jnp
from jax import lax
from jax.experimental import pallas as pl
from jax.experimental.pallas import tpu as pltpu
from jax.sharding import PartitionSpec as P

AH = 4
QB = 32
KW = 128
HALO = 64
HD = 48
LAST = 80
EPS = 1e-05
NEG = -1e30
BF = jnp.bfloat16
F32 = jnp.float32
MESH = pl.DeviceIdType.MESH
VMEM = pl.BlockSpec(memory_space=pltpu.VMEM)
SMEM = pl.BlockSpec(memory_space=pltpu.SMEM)
NT = (((1,), (1,)), ((), ()))


def layer_norm(values):
    centre = values - jnp.mean(values, axis=-1, keepdims=True)
    spread = jnp.mean(centre * centre, axis=-1, keepdims=True)
    return (centre * lax.rsqrt(spread + EPS)).astype(BF)


def dot(a, b):
    return jnp.dot(a, b, preferred_element_type=F32)


def iota(shape, dim):
    return lax.broadcasted_iota(jnp.int32, shape, dim)


def place():
    return lax.axis_index("atom"), lax.axis_index("row"), lax.axis_index("col")


def window(b, all_atoms, first_atom, start, query, pairs, bias_ref):
    width = query.shape[1]
    part = width // AH
    lane_head = iota((QB, width), 1) // part
    shift = start - (first_atom + QB * b) + HALO
    reach = pairs.shape[0]
    ahead = iota((KW, reach), 1) - iota((KW, reach), 0)
    pick = jnp.where(ahead == shift, 1.0, 0.0).astype(BF)
    keyed = dot(pick, pairs).astype(BF)
    stacked = jnp.concatenate(
        [jnp.where(lane_head == h, query, jnp.zeros_like(query)) for h in range(AH)], axis=0
    )
    scores = lax.dot_general(stacked, keyed[:, :width], NT, preferred_element_type=F32)
    bias = jnp.concatenate(
        [bias_ref[QB * b : QB * (b + 1), KW * h : KW * (h + 1)] for h in range(AH)], axis=0
    )
    scores = scores * part ** (-0.5) + bias.astype(F32)
    placed = start + iota((1, KW), 1)
    scores = jnp.where((placed >= 0) & (placed < all_atoms), scores, NEG)
    expo = jnp.exp(scores - jnp.max(scores, axis=-1, keepdims=True))
    weights = (expo / jnp.sum(expo, axis=-1, keepdims=True)).astype(BF)
    mixed = dot(weights, keyed[:, width:])
    block = mixed[:QB]
    for h in range(1, AH):
        block = jnp.where(lane_head == h, mixed[QB * h : QB * (h + 1)], block)
    return block


def tokens(member_ref, single_ref, hidden, device):
    toks, rows = single_ref.shape[0], hidden.shape[0]
    local = member_ref[...] - device * toks
    member = jnp.where(local == iota((toks, rows), 0), 1.0, 0.0)
    sums = dot(member.astype(BF), hidden)
    counts = jnp.sum(member, axis=1, keepdims=True)
    return layer_norm(single_ref[...].astype(F32) + sums / counts)


def chooser():
    span = 8 * HD
    source, target = iota((span, 512), 0), iota((span, 512), 1)
    lane = target % 128
    kind = (target // 128) % 2
    base = (target // 256) * 4 * HD
    first = base + jnp.where(kind == 0, 0, HD) + lane
    second = base + jnp.where(kind == 0, 3 * HD, 2 * HD) + lane - LAST
    wanted = jnp.where(lane < HD, first, jnp.where(lane >= LAST, second, -1))
    return jnp.where(source == wanted, 1.0, 0.0).astype(BF)


def tiles(head_data, choose, first, qg_ref, kv_ref):
    toks, columns = head_data.shape
    span = 8 * HD
    pairs = columns // span
    stacked = jnp.concatenate(
        [head_data[:, span * p : span * (p + 1)] for p in range(pairs)], axis=0
    )
    spread = dot(stacked, choose).astype(BF)
    for h in range(2 * pairs):
        rows_h = slice(toks * (h // 2), toks * (h // 2 + 1))
        at = 256 * (h % 2)
        qg_ref[first + h] = spread[rows_h, at : at + 128]
        kv_ref[first + h] = spread[rows_h, at + 128 : at + 256]


def summary(mixed, top):
    lane = iota(mixed.shape, 1)
    total = mixed[:, HD + 1 : HD + 2]
    high = top.astype(BF).astype(F32)
    middle = (top - high).astype(BF).astype(F32)
    total_high = total.astype(BF).astype(F32)
    for at, value in enumerate((high, middle, top - high - middle, total_high, total - total_high)):
        mixed = jnp.where(lane == 64 + at, value, mixed)
    return mixed


def paired(first, second):
    return jnp.where(iota(first.shape, 1) >= 64, first, pltpu.roll(second, 64, 1))


def merged(parts, gates):
    parts = [p.astype(F32) for p in parts]
    scales, totals = [], []
    for at in (64, 0):
        tops = [p[:, at : at + 1] + p[:, at + 1 : at + 2] + p[:, at + 2 : at + 3] for p in parts]
        counts = [p[:, at + 3 : at + 4] + p[:, at + 4 : at + 5] for p in parts]
        top = functools.reduce(jnp.maximum, tops)
        scales.append([jnp.exp(t - top) for t in tops])
        totals.append(sum(s * t for s, t in zip(scales[-1], counts)))
    low = iota(parts[0].shape, 1) >= 64
    mixed = sum(jnp.where(low, s, t) * p for s, t, p in zip(*scales, parts))
    attended = mixed / jnp.where(low, *totals) * jax.nn.sigmoid(gates)
    return jnp.transpose(attended).astype(BF)


def unless(own, remote, local):
    @pl.when(jnp.logical_not(own))
    def _():
        remote()

    @pl.when(own)
    def _():
        local()


def whole_kernel(
    all_atoms,
    start_ref,
    feats_in,
    w_atom_in,
    bias_in,
    w_atom_out_in,
    w_to_token_in,
    member_in,
    single_in,
    w_token_in,
    mask_in,
    pair_in,
    w_out_in,
    out_ref,
    feats_ref,
    w_atom_ref,
    bias_ref,
    w_atom_out_ref,
    w_to_token_ref,
    member_ref,
    single_ref,
    w_token_ref,
    mask_ref,
    pair_ref,
    w_out_ref,
    edge_ref,
    halo_ref,
    mixed_ref,
    qg_ref,
    kv_ref,
    qown_ref,
    kown_ref,
    qpack_ref,
    gate_ref,
    keys_ref,
    query_ref,
    peak_ref,
    score_ref,
    weight_ref,
    part_ref,
    got_ref,
    head_ref,
    all_ref,
    load,
    halo_send,
    halo_recv,
    send,
    q_sem,
    k_sem,
    g_send,
    gq_sem,
    gk_sem,
    gg_sem,
    m_send,
    m_recv,
    h_send,
    h_recv,
):
    a, r, c = place()
    n_atom, n_row, n_col = (lax.axis_size(x) for x in ("atom", "row", "col"))
    group_q, group_k = n_atom // n_row, n_atom // n_col
    devices = n_atom * n_row * n_col
    device = (a * n_row + r) * n_col + c
    rows = feats_ref.shape[0]
    barrier = pltpu.get_barrier_semaphore()
    loads = [
        pltpu.make_async_copy(source, target, load.at[i])
        for i, (source, target) in enumerate(
            (
                (feats_in, feats_ref),
                (w_atom_in, w_atom_ref),
                (bias_in, bias_ref),
                (w_atom_out_in, w_atom_out_ref),
                (w_to_token_in, w_to_token_ref),
                (member_in, member_ref),
                (single_in, single_ref),
                (w_token_in, w_token_ref),
                (mask_in, mask_ref),
                (pair_in, pair_ref),
                (w_out_in, w_out_ref),
            )
        )
    ]
    for copy in loads[:3]:
        copy.start()

    def signal(to):
        pl.semaphore_signal(barrier, inc=1, device_id=to, device_id_type=MESH)

    own_q = a // group_q == r
    own_k = a // group_k == c
    own_h = lax.rem(a, n_row) == c

    def greet(i, carry):
        signal((lax.rem(i + n_atom // 2 * (1 - a // (n_atom // 2)), n_atom), r, lax.rem(a, n_row)))
        signal((group_k * c + i // n_col, r, lax.rem(i, n_col)))
        signal((group_q * r + i // n_row, lax.rem(i, n_row), c))
        return carry

    lax.fori_loop(0, n_atom, greet, 0)
    for step in range(1, n_col):
        signal((a, r, lax.rem(c + step, n_col)))
    for step in range(1, n_row):
        signal((a, lax.rem(r + step, n_row), c))
    for step in (1, devices - 1):
        other = lax.rem(device + step, devices)
        signal((other // (n_row * n_col), lax.rem(other // n_col, n_row), lax.rem(other, n_col)))

    def halo_copy(side):
        other = lax.rem(device + (1 if side == 0 else devices - 1), devices)
        return pltpu.make_async_remote_copy(
            src_ref=edge_ref.at[side],
            dst_ref=halo_ref.at[side],
            send_sem=halo_send.at[side],
            recv_sem=halo_recv.at[side],
            device_id=(
                other // (n_row * n_col),
                lax.rem(other // n_col, n_row),
                lax.rem(other, n_col),
            ),
            device_id_type=MESH,
        )

    def drain_halo():
        for side in range(2):
            halo_copy(side).wait_send()

    for copy in loads[:3]:
        copy.wait()
    for copy in loads[3:9]:
        copy.start()
    rows, width = feats_ref.shape
    first_atom = device * rows
    with jax.named_scope("inner_windows"):
        feats = feats_ref[...]
        proj = dot(layer_norm(feats.astype(F32)), w_atom_ref[...])
        queries = proj[:, :width].astype(BF)
        pairs = proj[:, width : 3 * width].astype(BF)
        edge_ref[0] = pairs[rows - HALO :]
        edge_ref[1] = pairs[:HALO]
        gate = jax.nn.sigmoid(proj[:, 3 * width :])
        edge = HALO // QB
        blocks = rows // QB
        inner = range(edge, blocks - edge)

        def one_window(b, reach):
            query = queries[QB * b : QB * (b + 1)]
            mixed_ref[QB * b : QB * (b + 1)] = window(
                b, all_atoms, first_atom, start_ref[b], query, reach, bias_ref
            )

        for b in inner:
            one_window(b, pairs[QB * (b - edge) : QB * (b + edge + 1)])
    for copy in loads[9:]:
        copy.start()
    with jax.named_scope("barrier"):
        pl.semaphore_wait(barrier, 3 * n_atom + (n_col - 1) + (n_row - 1) + 2)
    with jax.named_scope("halo"):
        for side in range(2):
            halo_copy(side).start()
        for side in range(2):
            halo_copy(side).wait_recv()
    with jax.named_scope("outer_windows"):
        before, after = halo_ref[0], halo_ref[1]
        wide = jnp.concatenate([before, pairs[: QB * 2 * edge]], axis=0)
        for b in range(edge):
            one_window(b, wide[QB * b : QB * (b + 2 * edge + 1)])
        wide = jnp.concatenate([pairs[rows - QB * 2 * edge :], after], axis=0)
        for b in range(edge):
            one_window(blocks - edge + b, wide[QB * b : QB * (b + 2 * edge + 1)])
        gated = (mixed_ref[...] * gate).astype(BF)
    with jax.named_scope("tokens"):
        for copy in loads[3:7]:
            copy.wait()
        change = dot(gated, w_atom_out_ref[...])
        out_ref[:rows] = change.astype(BF)
        acted = (feats.astype(F32) + change).astype(BF)
        hidden = jnp.maximum(dot(acted, w_to_token_ref[...]), 0.0).astype(BF)
        normed = tokens(member_ref, single_ref, hidden, device)
        for copy in loads[7:9]:
            copy.wait()
        choose = chooser()

    q_four = lax.rem(a, group_q)
    q_slot = q_four * n_row + r
    k_four = lax.rem(a, group_k)
    k_slot = k_four * n_col + c

    def q_copy(to):
        return pltpu.make_async_remote_copy(
            src_ref=qg_ref.at[to],
            dst_ref=qown_ref.at[q_four, r],
            send_sem=send.at[0, to],
            recv_sem=q_sem.at[q_slot],
            device_id=(to, a // group_q, c),
            device_id_type=MESH,
        )

    def k_copy(to):
        return pltpu.make_async_remote_copy(
            src_ref=kv_ref.at[to],
            dst_ref=kown_ref.at[k_four, c],
            send_sem=send.at[1, to],
            recv_sem=k_sem.at[k_slot],
            device_id=(to, r, a // group_k),
            device_id_type=MESH,
        )

    def drain_tiles():
        def sent(to, carry):
            unless(own_q & (to == a), lambda: q_copy(to).wait_send(), lambda: None)
            unless(own_k & (to == a), lambda: k_copy(to).wait_send(), lambda: None)
            return carry

        lax.fori_loop(0, n_atom, sent, 0)

    half = n_atom // 2
    columns = half * 4 * HD
    for k in range(2):
        first = lax.rem(a // half + 1 + k, 2) * half
        with jax.named_scope("tiles"):
            span = pl.ds(pl.multiple_of(first * 4 * HD, 128), columns)
            head_data = dot(normed, w_token_ref[:, span]).astype(BF)
            tiles(head_data, choose, first, qg_ref, kv_ref)

        def start(i, carry):
            to = first + lax.rem(a + i, half)
            unless(
                own_q & (to == a),
                lambda: q_copy(to).start(),
                lambda: pltpu.make_async_copy(
                    qg_ref.at[to], qown_ref.at[q_four, r], q_sem.at[q_slot]
                ).start(),
            )
            unless(
                own_k & (to == a),
                lambda: k_copy(to).start(),
                lambda: pltpu.make_async_copy(
                    kv_ref.at[to], kown_ref.at[k_four, c], k_sem.at[k_slot]
                ).start(),
            )
            return carry

        with jax.named_scope("send_tiles"):
            lax.fori_loop(0, half, start, 0)

    def arrive_k(i, carry):
        pltpu.make_async_copy(
            kv_ref.at[0], kown_ref.at[i // n_col, lax.rem(i, n_col)], k_sem.at[i]
        ).wait()
        return carry

    def arrive_q(i, carry):
        pltpu.make_async_copy(
            qg_ref.at[0], qown_ref.at[i // n_row, lax.rem(i, n_row)], q_sem.at[i]
        ).wait()
        return carry

    def gather_q(step):
        return pltpu.make_async_remote_copy(
            src_ref=qpack_ref.at[c],
            dst_ref=qpack_ref.at[c],
            send_sem=g_send.at[0, step],
            recv_sem=gq_sem.at[step],
            device_id=(a, r, lax.rem(c + step, n_col)),
            device_id_type=MESH,
        )

    def gather_g(step):
        to = lax.rem(c + step, n_col)
        return pltpu.make_async_remote_copy(
            src_ref=qown_ref.at[:, to],
            dst_ref=gate_ref.at[:, c],
            send_sem=g_send.at[2, step],
            recv_sem=gg_sem.at[step],
            device_id=(a, r, to),
            device_id_type=MESH,
        )

    def partner(step):
        half = n_row // 2
        return lax.rem(r // 2 + step // 2, half) * 2 + lax.rem(lax.rem(r, 2) + step % 2, 2)

    def gather_k(step, value):
        mine = keys_ref.at[r, pl.ds(LAST if value else 0, HD)]
        return pltpu.make_async_remote_copy(
            src_ref=mine,
            dst_ref=mine,
            send_sem=g_send.at[3 + value, step],
            recv_sem=gk_sem.at[value, step],
            device_id=(a, partner(step), c),
            device_id_type=MESH,
        )

    def drain_gather():
        for step in range(1, n_col):
            gather_q(step).wait_send()
            gather_g(step).wait_send()
        for step in range(1, n_row):
            gather_k(step, 0).wait_send()
            gather_k(step, 1).wait_send()

    q_rows, keys = pair_ref.shape[1:]
    per_slot = q_rows // n_atom
    per_row = keys // n_row
    live = jnp.sum(jnp.sum(mask_ref[...], axis=0, keepdims=True), axis=1, keepdims=True)
    kind, column = iota((32, per_row), 0), iota((32, per_row), 1)
    token = (group_k * c + column // per_slot) * per_row + lax.rem(column, per_slot)
    for i in range(n_row):
        masked = jnp.where(token + i * per_slot < live, 0.0, NEG)
        extra = jnp.where(kind == 0, masked, jnp.where(kind == 1, 1.0, 0.0))
        keys_ref[i, HD:LAST] = extra.astype(BF)
    with jax.named_scope("tiles_arrive"):
        lax.fori_loop(0, n_atom, arrive_k, 0)
        moved = jnp.transpose(kown_ref[...].reshape(per_row, 128).astype(F32))
        keys_ref[r, :HD] = moved[:HD].astype(BF)
        keys_ref[r, LAST:] = moved[LAST:].astype(BF)
        for value in range(2):
            for step in range(1, n_row):
                gather_k(step, value).start()
        lax.fori_loop(0, n_atom, arrive_q, 0)
        half = q_rows // n_col // 2
        lane = iota((half, 128), 1)
        low = qown_ref[: group_q // 2].reshape(half, 128).astype(F32)
        high = qown_ref[group_q // 2 :].reshape(half, 128).astype(F32)
        qpack_ref[c] = jnp.where(lane < 64, low, pltpu.roll(high, 64, 1)).astype(BF)
        for step in (2, 1, 3):
            gather_q(step).start()
        for step in range(1, n_col):
            gather_g(step).start()
        gate_ref[:, c] = qown_ref[:, c]
    with jax.named_scope("gather_q"):
        wanted = lane < HD
        one = jnp.where(lane == HD, 1.0, 0.0)
        for step in range(n_col):
            source = lax.rem(c + n_col - step, n_col)
            if step > 0:
                gather_q(step).wait_recv()
            packed = qpack_ref[source].astype(F32)
            for i, value in enumerate((packed, pltpu.roll(packed, 64, 1))):
                value = jnp.where(wanted, value, one).astype(BF)
                slots = slice(n_atom // 2 * i, n_atom // 2 * (i + 1))
                query_ref[slots, source] = value.reshape(n_atom // 2, half * 2 // n_atom, 128)
    for copy in loads[9:]:
        copy.wait()
    peak_ref[...] = jnp.full_like(peak_ref, -jnp.inf)

    def score(step, carry):
        source = partner(step)

        @pl.when(step > 0)
        def _():
            mine = keys_ref.at[source, pl.ds(0, HD)]
            pltpu.make_async_copy(mine, mine, gk_sem.at[0, step]).wait()

        half = q_rows // 2
        span = half // (n_row * per_slot)
        for i in range(2):
            rows = slice(half * i, half * (i + 1))
            fours = slice(span * i, span * (i + 1))
            peak = peak_ref[fours]
            for at in range(0, per_row, 256):
                part = dot(
                    query_ref[n_atom // 2 * i : n_atom // 2 * (i + 1)].reshape(half, 128)[:, :LAST],
                    keys_ref[source, :LAST, at : at + 256],
                )
                for k in range(0, 256, 128):
                    four = (at + k) // 128
                    column = four * per_row + source * 128
                    bias = pair_ref[0, rows, pl.ds(pl.multiple_of(column, 128), 128)]
                    value = part[:, k : k + 128] * HD ** (-0.5) + bias.astype(F32)
                    value = value.reshape(peak.shape)
                    column = source * per_row + at + k
                    score_ref[fours, :, :, pl.ds(pl.multiple_of(column, 128), 128)] = value
                    peak = jnp.maximum(peak, value)
            peak_ref[fours] = peak
        return carry

    with jax.named_scope("scores"):
        lax.fori_loop(0, n_row, score, 0)

    def partial(step):
        to = lax.rem(c + step, n_col)
        return pltpu.make_async_remote_copy(
            src_ref=part_ref.at[to],
            dst_ref=got_ref.at[step],
            send_sem=m_send.at[step],
            recv_sem=m_recv.at[step],
            device_id=(a, r, to),
            device_id_type=MESH,
        )

    def drain_partials():
        for step in range(1, n_col):
            partial(step).wait_send()

    def quarter(i, carry):
        late = i // 2
        step = (1 - late) * (2 - i) + late * (i + 1)
        to = lax.rem(c + step, n_col)
        tops = [
            jnp.max(peak_ref[2 * h : 2 * h + 2, to].reshape(2 * per_slot, 128), axis=1, keepdims=True)
            for h in range(2)
        ]
        mixed = None
        for k in range(n_row):
            for h in range(2):
                for at in range(per_row * k, per_row * (k + 1), 256):
                    part = score_ref[2 * h : 2 * h + 2, to, :, at : at + 256]
                    part = jnp.exp(part.reshape(2 * per_slot, 256) - tops[h])
                    weight_ref[h, :, at : at + 256] = part.astype(BF)
            weights = weight_ref[:, :, per_row * k : per_row * (k + 1)]
            piece = lax.dot_general(
                weights.reshape(4 * per_slot, per_row),
                keys_ref[k],
                NT,
                preferred_element_type=F32,
            )
            mixed = piece if mixed is None else mixed + piece
        results = [
            summary(mixed[2 * per_slot * h : 2 * per_slot * (h + 1)], tops[h]) for h in range(2)
        ]
        part_ref[to] = paired(*results).astype(BF)

        @pl.when(i < n_col - 1)
        def _():
            partial(step).start()

        return carry

    with jax.named_scope("values_arrive"):
        for step in range(1, n_row):
            gather_k(step, 1).wait_recv()
    with jax.named_scope("attention"):
        lax.fori_loop(0, n_col, quarter, 0)
    with jax.named_scope("partials_arrive"):
        for step in range(1, n_col):
            partial(step).wait_recv()
            gather_g(step).wait_recv()

    def head_copy(j, k):
        return pltpu.make_async_remote_copy(
            src_ref=head_ref.at[j],
            dst_ref=all_ref.at[a],
            send_sem=h_send.at[j, k],
            recv_sem=h_recv.at[a],
            device_id=(n_row * j + c, r, lax.rem(c + k, n_col)),
            device_id_type=MESH,
        )

    def drain_heads():
        def sent(j, carry):
            for k in range(1, n_col):
                head_copy(j, k).wait_send()
            unless(
                own_h & (n_row * j + c == a),
                lambda: head_copy(j, 0).wait_send(),
                lambda: None,
            )
            return carry

        lax.fori_loop(0, group_k, sent, 0)

    out_rows = head_ref.shape[2]

    def one_head(i, carry):
        j = lax.rem(i + group_k // 2 * (1 - a // (n_atom // 2)), group_k)
        for k in (2, 1, 3):
            head_copy(j, k).start()
        unless(
            own_h & (n_row * j + c == a),
            lambda: head_copy(j, 0).start(),
            lambda: pltpu.make_async_copy(head_ref.at[j], all_ref.at[a], h_recv.at[a]).start(),
        )
        return carry

    with jax.named_scope("merge"):
        parts = [part_ref[c]] + [got_ref[step] for step in range(1, n_col)]
        gates = [
            jnp.concatenate(
                [gate_ref[u].reshape(per_slot, 128) for u in (2 * h, 2 * h + 1)], axis=0
            ).astype(F32)
            for h in range(2)
        ]
        attended = merged(parts, paired(*gates))
        for u in range(group_k):
            at = LAST - 64 * (u // 2)
            head_ref[u] = attended[at : at + HD, out_rows * (u % 2) : out_rows * (u % 2 + 1)]
    with jax.named_scope("send_heads"):
        lax.fori_loop(0, group_k, one_head, 0)

    def arrive(i, carry):
        pltpu.make_async_copy(head_ref.at[0], all_ref.at[i], h_recv.at[i]).wait()
        return carry

    with jax.named_scope("heads_arrive"):
        lax.fori_loop(0, n_atom, arrive, 0)
    with jax.named_scope("output"):
        heads = all_ref[...].reshape(n_atom * HD, head_ref.shape[2])
        out_ref[rows:] = dot(w_out_ref[...], heads).astype(BF)

    drain_halo()
    drain_tiles()
    drain_gather()
    drain_partials()
    drain_heads()


def split_kernel(both_ref, update_ref, out_ref):
    rows = update_ref.shape[0]
    update_ref[...] = both_ref[:rows]
    out_ref[...] = both_ref[rows:]


def shards(
    atom_feats,
    atom_to_token,
    window_start,
    atom_bias,
    token_single,
    token_mask,
    pair_bias,
    w_atom,
    w_atom_out,
    w_to_token,
    w_token,
    w_out,
):
    rows, width = atom_feats.shape
    toks = token_single.shape[0]
    axes = ("atom", "row", "col")
    n_atom, n_row, n_col = (lax.axis_size(x) for x in axes)
    devices = n_atom * n_row * n_col
    q_rows, k_cols = pair_bias.shape[1:]
    out_rows = q_rows // n_atom
    group = n_atom // n_col
    tile_rows = q_rows // n_col // 2
    operands = (
        atom_feats,
        w_atom,
        atom_bias,
        w_atom_out,
        w_to_token,
        atom_to_token.reshape(1, rows),
        token_single,
        w_token,
        token_mask.reshape(-1, 128),
        pair_bias,
        w_out.T,
    )
    dma = pltpu.SemaphoreType.DMA
    both = pl.pallas_call(
        functools.partial(whole_kernel, rows * devices),
        out_shape=jax.ShapeDtypeStruct((rows + w_out.shape[1], out_rows), BF),
        in_specs=[SMEM] + [pl.BlockSpec(memory_space=pl.ANY)] * len(operands),
        out_specs=VMEM,
        scratch_shapes=[pltpu.VMEM(x.shape, x.dtype) for x in operands]
        + [
            pltpu.VMEM((2, HALO, 2 * width), BF),
            pltpu.VMEM((2, HALO, 2 * width), BF),
            pltpu.VMEM((rows, width), F32),
            pltpu.VMEM((n_atom, toks, 128), BF),
            pltpu.VMEM((n_atom, toks, 128), BF),
            pltpu.VMEM((n_atom // n_row, n_row, toks, 128), BF),
            pltpu.VMEM((group, n_col, toks, 128), BF),
            pltpu.VMEM((n_col, tile_rows, 128), BF),
            pltpu.VMEM((group, n_col, toks, 128), BF),
            pltpu.VMEM((n_row, 128, k_cols // n_row), BF),
            pltpu.VMEM((n_atom, n_col, toks, 128), BF),
            pltpu.VMEM((group, n_row, out_rows, 128), F32),
            pltpu.VMEM((group, n_row, out_rows, k_cols), F32),
            pltpu.VMEM((2, tile_rows, k_cols), BF),
            pltpu.VMEM((n_col, tile_rows, 128), BF),
            pltpu.VMEM((n_col, tile_rows, 128), BF),
            pltpu.VMEM((group, HD, out_rows), BF),
            pltpu.VMEM((n_atom, HD, out_rows), BF),
            dma((len(operands),)),
            dma((2,)),
            dma((2,)),
            dma((2, n_atom)),
            dma((n_atom,)),
            dma((n_atom,)),
            dma((5, max(n_row, n_col))),
            dma((n_col,)),
            dma((2, n_row)),
            dma((n_col,)),
            dma((n_col,)),
            dma((n_col,)),
            dma((group, n_col)),
            dma((n_atom,)),
        ],
        compiler_params=pltpu.CompilerParams(
            collective_id=0, has_side_effects=True, vmem_limit_bytes=56 << 20
        ),
    )(window_start, *operands)
    update, flipped = pl.pallas_call(
        split_kernel,
        out_shape=(
            jax.ShapeDtypeStruct((rows, width), BF),
            jax.ShapeDtypeStruct((w_out.shape[1], out_rows), BF),
        ),
        in_specs=[VMEM],
        out_specs=(VMEM, VMEM),
    )(both)
    return (update, flipped.T)


def solution(mesh):
    placed = (
        P(("atom", "row", "col"), None),
        P(("atom", "row", "col")),
        P(("atom", "row", "col")),
        P(("atom", "row", "col"), None),
        P(("atom", "row", "col"), None),
        P(),
        P("atom", "row", "col"),
        P(),
        P(),
        P(),
        P(),
        P(None, "col"),
    )
    return jax.shard_map(
        shards,
        mesh=mesh,
        in_specs=placed,
        out_specs=(P(("atom", "row", "col"), None), P(("row", "atom"), "col")),
        check_vma=False,
    )
```
